512 devices in a mesh: ka: 8 (over z), pb: 64 (over y, x, core).
Axes of the slice: x: 4, y: 8, z: 8, core: 2. Of those that a mesh axis runs over, the one named last changes fastest.
Arguments:
- wannier_g: bfloat16 [8, 1920, 13824], P('ka', 'pb'), may hold values from -0.125 to 0.125
- rotations: float32 [512, 512], P(('ka', 'pb')), may hold values from -1 to 1
- home_rows: int32 [512], replicated, may hold values from 0 to 511, each once
- shifted: int32 [8, 512], P('ka', 'pb'), may hold values from 0 to 511, as said below
- band_count: int32 [8, 512], P('ka', 'pb'), may hold values from 4 to 16
- lattice: int32 [3, 1920], replicated, may hold values from -6 to 6
Outputs:
- bloch_g: bfloat16 [8, 512, 13824], P('ka', 'pb')
The draws below stay inside these ranges and needn't reach their ends.
Inputs may be any that keep to these rules, and one draw needn't show every extreme that they name: shifted[q, k] is the fine point whose grid coordinates are those of k plus those of one fine point drawn for q, modulo 8. `home_rows`: each fine point is held by exactly one row.
All inputs are finite; a program needn't handle non-finite values.
Results may differ from the reference program's by a relative error of at most 0.0049.
Values may be sent and summed in bfloat16 or wider, within the bound.
A program may use at most 64 MiB of HBM per device.

```python
import jax
import jax.numpy as jnp
from jax import lax

NW = 16
NMODE = 27
NR = 1920
NKG = 8
K = 512
Q = 8


def draw_shifted(key, part):
    key = jax.random.fold_in(key, 5)
    offsets = jax.random.randint(key, (Q,), 0, K)
    points = jnp.arange(K, dtype=jnp.int32)
    first_coord = (points[None, :] // (NKG * NKG) + offsets[:, None] // (NKG * NKG)) % NKG
    second_coord = (points[None, :] // NKG % NKG + offsets[:, None] // NKG % NKG) % NKG
    third_coord = (points[None, :] % NKG + offsets[:, None] % NKG) % NKG
    return (first_coord * NKG * NKG + second_coord * NKG + third_coord).astype(jnp.int32)


def touch_ends(result, own_key, low, top_value):
    extent = result.shape
    index_at = [jax.random.randint(jax.random.fold_in(own_key, axis), (), 0, extent[axis]) for axis in range(len(extent))]
    result = result.at[tuple(index_at)].set(low)
    longest = extent.index(max(extent))
    index_at[longest] = (index_at[longest] + 1) % extent[longest]
    return result.at[tuple(index_at)].set(top_value)


def steps_of(stream_key, dims, cuts, least, high):
    gain, own = 1.0, jax.random.fold_in(stream_key, 6)
    for position, parts in cuts:
        heights = jnp.exp(jax.random.uniform(jax.random.fold_in(own, position), (parts,), jnp.float32, least / len(cuts), high / len(cuts)))
        gain = gain * jnp.repeat(heights, dims[position] // parts).reshape([-1 if axis == position else 1 for axis in range(len(dims))])
    return gain


def gaussian(own_key, dims, scale, bound, split=(), kind=jnp.bfloat16):
    loudness = steps_of(own_key, dims, split, -0.22, 0.18) if split else 1.0
    array = jax.random.normal(own_key, dims, jnp.float32) * scale * loudness
    return jnp.minimum(jnp.maximum(array, -bound), bound).astype(kind)


def setup_inputs(seed: int = 0) -> dict:
    streams_of = jax.random.split(jax.random.key(seed), 7)
    return {
        "wannier_g": gaussian(streams_of[0], (Q, NR, NW * NW * NMODE * 2), NR ** -0.5, 0.125, ((0, 8), (1, 64))),
        "rotations": gaussian(streams_of[1], (K, NW * NW * 2), 0.18, 1.0, ((0, 512),), jnp.float32),
        "home_rows": jax.random.permutation(streams_of[2], K).astype(jnp.int32),
        "shifted": draw_shifted(jax.random.fold_in(streams_of[6], 71), 0),
        "band_count": touch_ends(jax.random.randint(streams_of[4], (Q, K), 4, NW + 1), jax.random.fold_in(streams_of[4], 1), 4, NW).astype(jnp.int32),
        "lattice": touch_ends(jax.random.randint(streams_of[5], (3, NR), -6, 7), jax.random.fold_in(streams_of[5], 1), -6, 6).astype(jnp.int32),
    }


def phase_table(lattice):
    points = jnp.arange(K, dtype=jnp.int32)
    first_coord = points // (NKG * NKG)
    second_coord = (points // NKG) % NKG
    third_coord = points % NKG
    winding = first_coord[:, None] * lattice[0][None, :] + second_coord[:, None] * lattice[1][None, :] + third_coord[:, None] * lattice[2][None, :]
    winding = jnp.mod(winding, NKG)
    angles = winding.astype(jnp.float32) * (2.0 * jnp.pi / NKG)
    return jnp.concatenate([jnp.cos(angles), jnp.sin(angles)], axis=0).astype(jnp.bfloat16)


def combine(summed):
    leading = summed.shape[:-2]
    points = summed.shape[-2] // 2
    width = summed.shape[-1]
    halves = summed.reshape(leading + (2, points, width // 2, 2))
    cosine = halves[..., 0, :, :, :]
    sine_part = halves[..., 1, :, :, :]
    real_out = cosine[..., 0] - sine_part[..., 1]
    imag_out = sine_part[..., 0] + cosine[..., 1]
    return jnp.stack([real_out, imag_out], axis=-1).reshape(leading + (points, width)).astype(jnp.bfloat16)


def rotate(tiles, rot_right, rot_left, counts):
    def contract(form, first_op, second_op):
        return jnp.einsum(form, first_op, second_op, precision=lax.Precision.HIGHEST)
    real_tile, imag_tile = tiles[..., 0], tiles[..., 1]
    real_right, imag_right = rot_right[..., 0], rot_right[..., 1]
    real_left, imag_left = rot_left[..., 0], rot_left[..., 1]
    first_form = "...mnv,...nj->...mjv"
    real_mid = contract(first_form, real_tile, real_right) - contract(first_form, imag_tile, imag_right)
    imag_mid = contract(first_form, real_tile, imag_right) + contract(first_form, imag_tile, real_right)
    second_form = "...mi,...mjv->...ijv"
    real_out = contract(second_form, real_left, real_mid) + contract(second_form, imag_left, imag_mid)
    imag_out = contract(second_form, real_left, imag_mid) - contract(second_form, imag_left, real_mid)
    band_index = jnp.arange(NW, dtype=jnp.int32)
    limit = counts[..., None, None]
    inside = (band_index[:, None] < limit) & (band_index[None, :] < limit)
    inside = inside[..., None]
    zeros = jnp.zeros_like(real_out)
    return jnp.stack([jnp.where(inside, real_out, zeros), jnp.where(inside, imag_out, zeros)], axis=-1)


def reference(wannier_g, rotations, home_rows, shifted, band_count, lattice):
    phases = phase_table(lattice).astype(jnp.float32)
    blocks = jnp.zeros_like(rotations).at[home_rows].set(rotations).reshape(K, NW, NW, 2)

    def one_point(operands):
        wannier_slab, targets, counts = operands
        summed = jnp.dot(phases, wannier_slab.astype(jnp.float32), precision=lax.Precision.HIGHEST, preferred_element_type=jnp.float32)
        rounded = lax.optimization_barrier(combine(summed))
        tiles = rounded.astype(jnp.float32).reshape(K, NW, NW, NMODE, 2)
        rotated = rotate(tiles, blocks, blocks[targets], counts)
        return rotated.reshape(K, NW * NW * NMODE * 2).astype(jnp.bfloat16)

    return lax.map(one_point, (wannier_g, shifted, band_count))
```

```python
import jax
import jax.numpy as jnp
from jax import lax
from jax.experimental import pallas as pl
from jax.experimental.pallas import tpu as pltpu
from jax.sharding import PartitionSpec as P

NW = 16
NKG = 8
K = 512
VEC = 54
ROWS = 30
PB = 64
KA = 8
WORKERS = 54
COLS = 256
MESH = pl.DeviceIdType.MESH
F32 = jnp.float32
BF16 = jnp.bfloat16
HALF_ROOT = 0.70703125
CUBIC = (0.5 - HALF_ROOT) / 3.0
LINEAR = HALF_ROOT - CUBIC


def worker_index(d):
    return (27 * d + 31) // 32


def is_worker(d):
    return (32 * worker_index(d)) // 27 == d


def y_step(i):
    odd = i % 2
    return odd * ((i + 1) // 2) + (1 - odd) * ((8 - i // 2) % 8)


def iota(shape, axis):
    return lax.broadcasted_iota(jnp.int32, shape, axis)


def swap_parts(x):
    width = x.shape[1]
    even = iota(x.shape, 1) % 2 == 0
    return jnp.where(even, -pltpu.roll(x, width - 1, axis=1), pltpu.roll(x, 1, axis=1))


def wave(t):
    w = (jnp.abs((t & 7) - 4) - 2).astype(F32)
    return w * (LINEAR + CUBIC * (w * w))


def comm_kernel(
    g, rot, home, shifted, lattice, blk_out, lhs1_out, lhs2_out,
    recv1, xg, acc, cosp, sinp, send2, recv2, ya, xb, zc, lat, third, lh, ll,
    g_send, g_recv, b_send, b_recv, y_send, y_recv, x_send, x_recv, z_send, z_recv, c_send, c_recv,
):
    za = lax.axis_index("ka")
    me = lax.axis_index("pb")
    yy = me // 8
    xc = me % 8
    xx = xc // 2
    cc = xc % 2
    barrier = pltpu.get_barrier_semaphore()

    def greet(s, carry):
        pl.semaphore_signal(barrier, inc=1, device_id={"pb": (me + s) % PB}, device_id_type=MESH)
        return carry

    lax.fori_loop(1, PB, greet, 0)

    def greet_z(s, carry):
        pl.semaphore_signal(barrier, inc=1, device_id={"ka": (za + s) % KA}, device_id_type=MESH)
        return carry

    lax.fori_loop(1, KA, greet_z, 0)

    lane3 = iota((3, 128), 1)
    for tile in range(16):
        a, off = (120 * tile) // 128, (120 * tile) % 128
        b = min(a + 1, 14)
        first, second = lattice[:, 128 * a : 128 * a + 128], lattice[:, 128 * b : 128 * b + 128]
        out = jnp.zeros((3, 128), jnp.int32)
        for c in range(4):
            shift = (2 * c - off) % 128
            here, there = first, second
            if shift:
                here, there = pltpu.roll(first, shift, axis=1), pltpu.roll(second, shift, axis=1)
            value = jnp.where(lane3 < 128 - off + 2 * c, here, there)
            out = jnp.where(lane3 // 32 == c, value, out)
        lat[:, 128 * tile : 128 * tile + 128] = out
    third[...] = iota((8, 2048), 0) * lat[2:3, :]
    xg[...] = jnp.zeros_like(xg)
    ya[yy] = rot[...]

    pl.semaphore_wait(barrier, PB - 1 + KA - 1)

    def y_copy(s):
        peer = (yy + s) % 8
        return pltpu.make_async_remote_copy(
            rot, ya.at[yy], y_send.at[s], y_recv.at[yy],
            device_id={"pb": peer * 8 + xc}, device_id_type=MESH)

    def y_start(s, carry):
        y_copy(s).start()
        return carry

    lax.fori_loop(1, 8, y_start, 0)

    def g_copy(d):
        cols = pl.ds(pl.multiple_of(worker_index(d) * COLS, COLS), COLS)
        return pltpu.make_async_remote_copy(
            g.at[0, :, cols], recv1.at[me], g_send.at[d], g_recv.at[me],
            device_id={"pb": d}, device_id_type=MESH)

    def g_own():
        cols = pl.ds(pl.multiple_of(worker_index(me) * COLS, COLS), COLS)
        return pltpu.make_async_copy(g.at[0, :, cols], recv1.at[me], g_recv.at[me])

    @pl.when(is_worker(me))
    def _():
        g_own().start()

    def partner(s):
        return ((yy + y_step(s // 8)) % 8) * 8 + (xc + s) % 8

    def g_start(s, carry):
        d = partner(s)

        @pl.when(is_worker(d))
        def _():
            g_copy(d).start()

        return carry

    lax.fori_loop(1, PB, g_start, 0)

    def phases(b, carry):
        first = (b // 4) * lat[0:1, :]
        second = lat[1:2, :]
        k2 = (b % 4) * 2
        low = (first + k2 * second) + third[...]
        high = (first + (k2 + 1) * second) + third[...]
        t = jnp.concatenate([low, high], axis=0)
        rows = pl.ds(pl.multiple_of(b * 16, 16), 16)
        cosp[rows, :] = wave(t).astype(BF16)
        sinp[rows, :] = wave(t + 6).astype(BF16)
        return carry

    lax.fori_loop(0, 8, phases, 0)

    def y_wait(s, carry):
        src = (yy + s) % 8
        pltpu.make_async_remote_copy(
            rot, ya.at[src], y_send.at[s], y_recv.at[src],
            device_id={"pb": src * 8 + xc}, device_id_type=MESH).wait_recv()
        return carry

    lax.fori_loop(1, 8, y_wait, 0)

    def x_copy(s, slot):
        peer = (xx + s) % 4
        return pltpu.make_async_remote_copy(
            ya, xb.at[pl.ds(8 * slot, 8)], x_send.at[s], x_recv.at[slot],
            device_id={"pb": yy * 8 + peer * 2 + cc}, device_id_type=MESH)

    for s in range(1, 4):
        x_copy(s, xx).start()
    xb[pl.ds(8 * xx, 8)] = ya[...]

    lax.fori_loop(8, 20, phases, 0)

    for s in range(1, 4):
        x_copy(s, (xx + s) % 4).wait_recv()

    def z_copy(s, slot):
        return pltpu.make_async_remote_copy(
            xb, zc.at[pl.ds((cc * 8 + slot) * 32, 32)], z_send.at[s], z_recv.at[slot],
            device_id={"ka": (za + s) % KA}, device_id_type=MESH)

    def z_start(s, carry):
        z_copy(s, za).start()
        return carry

    lax.fori_loop(1, KA, z_start, 0)
    zc[pl.ds((cc * 8 + za) * 32, 32)] = xb[...]

    lax.fori_loop(20, 32, phases, 0)

    def group(i, carry):
        ys = (yy - y_step(i) + 8) % 8

        def arrive(u, inner):
            src = ys * 8 + u

            @pl.when(src == me)
            def _():
                g_own().wait()

            @pl.when(src != me)
            def _():
                pltpu.make_async_remote_copy(
                    g.at[0, :, pl.ds(0, COLS)], recv1.at[src], g_send.at[src], g_recv.at[src],
                    device_id={"pb": src}, device_id_type=MESH).wait_recv()

            return inner

        lax.fori_loop(0, 8, arrive, 0)
        for u in range(8):
            xg[u, 0:ROWS, :] = recv1[ys * 8 + u]
        x = xg[...].reshape(256, COLS)
        x_swapped = swap_parts(x.astype(F32)).astype(BF16)
        lanes = pl.ds(pl.multiple_of(ys * 256, 256), 256)
        total = jnp.dot(cosp[:, lanes], x, preferred_element_type=F32)
        total += jnp.dot(sinp[:, lanes], x_swapped, preferred_element_type=F32)
        acc[...] += total
        return carry

    @pl.when(is_worker(me))
    def _():
        acc[...] = jnp.zeros_like(acc)
        lax.fori_loop(0, 5, group, 0)

    def z_wait(s, carry):
        z_copy(s, (za + s) % KA).wait_recv()
        return carry

    lax.fori_loop(1, KA, z_wait, 0)

    def c_copy(half):
        part = zc.at[pl.ds(half * 256, 256)]
        return pltpu.make_async_remote_copy(
            part, part, c_send.at[0], c_recv.at[0],
            device_id={"pb": me + 1 - 2 * cc}, device_id_type=MESH)

    c_copy(cc).start()

    def b_copy(d):
        return pltpu.make_async_remote_copy(
            send2.at[d], recv2.at[worker_index(me)], b_send.at[d], b_recv.at[worker_index(me)],
            device_id={"pb": d}, device_id_type=MESH)

    def b_own():
        return pltpu.make_async_copy(send2.at[me], recv2.at[worker_index(me)], b_recv.at[worker_index(me)])

    @pl.when(is_worker(me))
    def _():
        lax.fori_loop(5, 8, group, 0)

        def pack(s, carry):
            d = partner(s)
            rows = acc[pl.ds(pl.multiple_of(8 * d, 8), 8), :]
            send2[d] = jnp.concatenate([rows[:, :128], rows[:, 128:]], axis=0).astype(BF16)

            @pl.when(d != me)
            def _():
                b_copy(d).start()

            @pl.when(d == me)
            def _():
                b_own().start()

            return carry

        lax.fori_loop(0, PB, pack, 0)

    c_copy(1 - cc).wait_recv()
    r = iota((1, K), 1)
    place = (((r % 2) * 8 + r // 64) * 4 + (r // 2) % 4) * 8 + (r // 8) % 8
    sub = iota((8, K), 0)
    own = jnp.zeros((8, K), F32)
    other = jnp.zeros((8, K), F32)
    for k in range(8):
        at = jnp.minimum(jnp.sum(jnp.where(home[...] == me * 8 + k, place, 0)), K - 1)
        own = jnp.where(sub == k, zc[at], own)
        at = jnp.minimum(jnp.sum(jnp.where(home[...] == shifted[0, k], place, 0)), K - 1)
        other = jnp.where(sub == k, zc[at], other)
    both = jnp.concatenate([own, other], axis=0)
    for jp in range(32):
        pieces = [both[:, 128 * v : 128 * v + 128] for v in range(4)]
        if jp:
            pieces = [pltpu.roll(piece, 128 - jp, axis=1) for piece in pieces]
        turned = jnp.concatenate(pieces, axis=1)
        upper = turned.astype(BF16)
        lh[16 * jp : 16 * jp + 16, :] = upper
        ll[16 * jp : 16 * jp + 16, :] = (turned - upper.astype(F32)).astype(BF16)
    spread = jnp.where(iota((K, 128), 0) == 32 * (iota((K, 128), 1) // 8), 1.0, 0.0).astype(BF16)
    keep = iota((K, 128), 1) % 8 == iota((K, 128), 0) % 8
    for level, source in ((0, lh), (1, ll)):
        full = jnp.where(keep, jnp.dot(source[...], spread, preferred_element_type=F32), 0.0)
        for jj in range(8):
            for part in range(2):
                a = 16 * (4 * jj + part)
                b = 16 * (4 * jj + 2 + part)
                rows = slice(128 * level + 16 * jj, 128 * level + 16 * jj + 16)
                lanes = slice(128 * part, 128 * part + 128)
                lhs1_out[rows, lanes] = jnp.concatenate([full[a : a + 8], full[b : b + 8]], axis=0).astype(BF16)
                left = jnp.concatenate([full[a + 8 : a + 16], full[b + 8 : b + 16]], axis=0)
                lhs2_out[rows, lanes] = (left if part == 0 else -left).astype(BF16)

    def b_wait(j, carry):
        d = (32 * j) // 27

        @pl.when(d == me)
        def _():
            b_own().wait()

        @pl.when(d != me)
        def _():
            pltpu.make_async_remote_copy(
                send2.at[d], recv2.at[j], b_send.at[d], b_recv.at[j],
                device_id={"pb": d}, device_id_type=MESH).wait_recv()

        return carry

    lax.fori_loop(0, WORKERS, b_wait, 0)
    blk_out[...] = recv2[...]

    def y_left(s, carry):
        y_copy(s).wait_send()
        return carry

    lax.fori_loop(1, 8, y_left, 0)
    for s in range(1, 4):
        x_copy(s, xx).wait_send()

    def z_left(s, carry):
        z_copy(s, za).wait_send()
        return carry

    lax.fori_loop(1, KA, z_left, 0)
    c_copy(cc).wait_send()

    def g_left(s, carry):
        d = partner(s)

        @pl.when(is_worker(d))
        def _():
            g_copy(d).wait_send()

        return carry

    lax.fori_loop(1, PB, g_left, 0)

    @pl.when(is_worker(me))
    def _():
        def b_left(s, carry):
            b_copy(partner(s)).wait_send()
            return carry

        lax.fori_loop(1, PB, b_left, 0)


def rotate_kernel(blk, lhs1, lhs2, counts, out, padded, middle, final):
    lane = iota((8, 128), 1)
    low_half = lane < 64

    def compact_tile(t):
        return blk[t // 2].astype(F32)[8 * (t % 2) : 8 * (t % 2) + 8]

    tiles = [compact_tile(t) for t in range(108)]

    def turn(x, shift):
        shift %= 128
        return pltpu.roll(x, shift, axis=1) if shift else x

    for n in range(NW):
        for mp in range(8):
            halves = []
            for h in range(2):
                start = VEC * (16 * (2 * mp + h) + n)
                t, off = start // 128, start % 128
                piece = turn(tiles[t], 64 * h - off)
                if off + VEC > 128:
                    spill = turn(tiles[t + 1], 64 * h - off)
                    piece = jnp.where(lane < 128 - off + 64 * h, piece, spill)
                halves.append(piece)
            padded[8 * n : 8 * n + 8, 128 * mp : 128 * mp + 128] = jnp.where(low_half, halves[0], halves[1])

    for p in range(4):
        lanes = slice(256 * p, 256 * p + 256)
        x = padded[:, lanes]
        rhs = jnp.concatenate([x, swap_parts(x)], axis=0).astype(BF16)
        both = jnp.dot(lhs1[...], rhs, preferred_element_type=F32)
        middle[:, lanes] = both[:128] + both[128:]

    for a in range(8):
        for b in range(8):
            lanes = slice(128 * b, 128 * b + 128)
            first = middle[16 * a : 16 * a + 8, lanes]
            second = middle[16 * a + 8 : 16 * a + 16, lanes]
            place = slice(128 * a, 128 * a + 128)
            padded[16 * b : 16 * b + 8, place] = jnp.where(low_half, first, turn(second, 64))
            padded[16 * b + 8 : 16 * b + 16, place] = jnp.where(low_half, turn(first, 64), second)

    sub = iota((8, 1), 0)
    limit = jnp.zeros((8, 1), jnp.int32)
    for k in range(8):
        limit = jnp.where(sub == k, counts[0, k], limit)
    row = iota((128, 256), 0)
    limits = jnp.concatenate([jnp.broadcast_to(limit, (8, 256))] * 16, axis=0)
    for p in range(4):
        lanes = slice(256 * p, 256 * p + 256)
        x = padded[:, lanes]
        x = jnp.concatenate([x, swap_parts(x)], axis=0)
        upper = x.astype(BF16)
        lower = (x - upper.astype(F32)).astype(BF16)
        both = jnp.dot(lhs2[...], upper, preferred_element_type=F32)
        total = both[:128] + (both[128:] + jnp.dot(lhs2[:128, :], lower, preferred_element_type=F32))
        band = jnp.maximum(row // 8, 4 * p + iota((128, 256), 1) // 64)
        final[:, lanes] = jnp.where(band < limits, total, 0.0)

    for t in range(108):
        begin = 128 * t
        value = None
        for q in range(begin // VEC, (begin + 127) // VEC + 1):
            if q >= 256:
                continue
            i, j = q // 16, q % 16
            at = VEC * q - begin
            piece = turn(final[8 * i : 8 * i + 8, 128 * (j // 2) : 128 * (j // 2) + 128], at - 64 * (j % 2))
            value = piece if value is None else jnp.where(lane < at, value, piece)
        out[0, :, begin : begin + 128] = value.astype(BF16)


def per_device(wannier_g, rotations, home_rows, shifted, band_count, lattice):
    vmem = pl.BlockSpec(memory_space=pltpu.VMEM)
    smem = pl.BlockSpec(memory_space=pltpu.SMEM)
    dma = pltpu.SemaphoreType.DMA
    blocks, lhs1, lhs2 = pl.pallas_call(
        comm_kernel,
        out_shape=(
            jax.ShapeDtypeStruct((WORKERS, 16, 128), BF16),
            jax.ShapeDtypeStruct((256, 256), BF16),
            jax.ShapeDtypeStruct((256, 256), BF16),
        ),
        in_specs=[pl.BlockSpec(memory_space=pl.ANY), vmem, vmem, smem, vmem],
        out_specs=(vmem, vmem, vmem),
        scratch_shapes=[
            pltpu.VMEM((PB, ROWS, COLS), BF16),
            pltpu.VMEM((8, 32, COLS), BF16),
            pltpu.VMEM((K, COLS), F32),
            pltpu.VMEM((K, 2048), BF16),
            pltpu.VMEM((K, 2048), BF16),
            pltpu.VMEM((PB, 16, 128), BF16),
            pltpu.VMEM((WORKERS, 16, 128), BF16),
            pltpu.VMEM((8, 1, 512), F32),
            pltpu.VMEM((32, 1, 512), F32),
            pltpu.VMEM((512, 1, 512), F32),
            pltpu.VMEM((3, 2048), jnp.int32),
            pltpu.VMEM((8, 2048), jnp.int32),
            pltpu.VMEM((K, 512), BF16),
            pltpu.VMEM((K, 512), BF16),
            dma((PB,)), dma((PB,)), dma((PB,)), dma((WORKERS,)),
            dma((8,)), dma((8,)), dma((4,)), dma((4,)), dma((8,)), dma((8,)), dma((1,)), dma((1,)),
        ],
        compiler_params=pltpu.CompilerParams(
            collective_id=0, has_side_effects=True, vmem_limit_bytes=40 * 1024 * 1024
        ),
        name="exchange",
    )(wannier_g, rotations, home_rows.reshape(1, K), shifted, lattice)
    return pl.pallas_call(
        rotate_kernel,
        out_shape=jax.ShapeDtypeStruct((1, 8, NW * NW * VEC), BF16),
        in_specs=[vmem, vmem, vmem, smem],
        out_specs=vmem,
        scratch_shapes=[
            pltpu.VMEM((128, 1024), F32),
            pltpu.VMEM((128, 1024), F32),
            pltpu.VMEM((128, 1024), F32),
        ],
        compiler_params=pltpu.CompilerParams(vmem_limit_bytes=32 * 1024 * 1024),
        name="rotate",
    )(blocks, lhs1, lhs2, band_count)


def solution(mesh):
    placed = (P("ka", "pb", None), P(("ka", "pb"), None), P(), P("ka", "pb"), P("ka", "pb"), P())
    return jax.shard_map(
        per_device, mesh=mesh, in_specs=placed, out_specs=P("ka", "pb", None), check_vma=False
    )
```

```python
import jax
import jax.numpy as jnp
from jax import lax
from jax.experimental import pallas as pl
from jax.experimental.pallas import tpu as pltpu
from jax.sharding import PartitionSpec as P

NW = 16
NKG = 8
K = 512
VEC = 54
ROWS = 30
PB = 64
KA = 8
Y_ORDER = (0, 1, 7, 2, 6, 3, 5, 4)
WORKERS = 54
COLS = 256
MESH = pl.DeviceIdType.MESH
F32 = jnp.float32
BF16 = jnp.bfloat16
HALF_ROOT = 0.70703125
CUBIC = (0.5 - HALF_ROOT) / 3.0
LINEAR = HALF_ROOT - CUBIC


def worker_index(d):
    return (27 * d + 31) >> 5


def is_worker(d):
    return ((5 * d) & 31) < 27


def iota(shape, axis):
    return lax.broadcasted_iota(jnp.int32, shape, axis)


def swap_parts(x):
    width = x.shape[1]
    even = iota(x.shape, 1) % 2 == 0
    return jnp.where(even, -pltpu.roll(x, width - 1, axis=1), pltpu.roll(x, 1, axis=1))


def wave(t):
    w = (jnp.abs((t & 7) - 4) - 2).astype(F32)
    return w * (LINEAR + CUBIC * (w * w))


def comm_kernel(
    g, rot_hbm, home_hbm, shifted_hbm, lattice_hbm, blk_out, lhs1_out, lhs2_out,
    rot, home, shifted, lattice, recv1, xg, acc, cosp, sinp, send2, ya, xb, zc, lat, third, lh, ll, lhs1, lhs2,
    in_sem, g_send, g_recv, b_send, b_recv, y_send, y_recv, x_send, x_recv, z_send, z_recv, c_send, c_recv, out_sem,
):
    za = lax.axis_index("ka")
    me = lax.axis_index("pb")
    yy = me >> 3
    xc = me & 7
    xx = xc >> 1
    cc = xc & 1
    working = is_worker(me)
    barrier = pltpu.get_barrier_semaphore()
    reads = [
        pltpu.make_async_copy(source, target, in_sem.at[i])
        for i, (source, target) in enumerate(
            ((lattice_hbm, lattice), (rot_hbm, rot), (home_hbm, home), (shifted_hbm, shifted)))
    ]
    for read in reads:
        read.start()

    def greet(s, carry):
        pl.semaphore_signal(barrier, inc=1, device_id=(za, me ^ s), device_id_type=MESH)
        return carry

    lax.fori_loop(1, PB, greet, 0)

    def greet_z(s, carry):
        pl.semaphore_signal(barrier, inc=1, device_id=(za ^ s, me), device_id_type=MESH)
        return carry

    lax.fori_loop(1, KA, greet_z, 0)

    for read in reads:
        read.wait()

    lane3 = iota((3, 128), 1)
    for tile in range(16):
        a, off = (120 * tile) // 128, (120 * tile) % 128
        b = min(a + 1, 14)
        first, second = lattice[:, 128 * a : 128 * a + 128], lattice[:, 128 * b : 128 * b + 128]
        out = jnp.zeros((3, 128), jnp.int32)
        for c in range(4):
            shift = (2 * c - off) % 128
            here, there = first, second
            if shift:
                here, there = pltpu.roll(first, shift, axis=1), pltpu.roll(second, shift, axis=1)
            value = jnp.where(lane3 < 128 - off + 2 * c, here, there)
            out = jnp.where(lane3 // 32 == c, value, out)
        lat[:, 128 * tile : 128 * tile + 128] = out
    third[...] = iota((8, 2048), 0) * lat[2:3, :]
    xg[...] = jnp.zeros_like(xg)
    ya[yy] = rot[...]

    def phases(b, carry):
        first = (b >> 2) * lat[0:1, :]
        second = lat[1:2, :]
        k2 = (b & 3) * 2
        low = (first + k2 * second) + third[...]
        high = (first + (k2 + 1) * second) + third[...]
        t = jnp.concatenate([low, high], axis=0)
        rows = pl.ds(pl.multiple_of(b * 16, 16), 16)
        cosp[rows, :] = wave(t).astype(BF16)
        sinp[rows, :] = wave(t + 6).astype(BF16)
        return carry

    pl.semaphore_wait(barrier, PB - 1 + KA - 1)

    def y_copy(s):
        peer = (yy + s) & 7
        return pltpu.make_async_remote_copy(
            rot, ya.at[yy], y_send.at[s], y_recv.at[yy],
            device_id=(za, peer * 8 + xc), device_id_type=MESH)

    def y_start(s, carry):
        y_copy(s).start()
        return carry

    lax.fori_loop(1, 8, y_start, 0)

    def g_columns(d):
        return g.at[0, :, pl.ds(pl.multiple_of(worker_index(d) * COLS, COLS), COLS)]

    @pl.when(working)
    def _():
        pltpu.make_async_copy(g_columns(me), recv1.at[me], g_recv.at[yy]).start()

    def g_start(step):
        base = ((yy + step) & 7) * 8

        def one(u, carry):
            d = base + (xc ^ u)

            @pl.when(is_worker(d))
            def _():
                pltpu.make_async_remote_copy(
                    g_columns(d), recv1.at[me], g_send.at[0], g_recv.at[yy],
                    device_id=(za, d), device_id_type=MESH).start()

            return carry

        lax.fori_loop(0 if step else 1, 8, one, 0)

    for step in Y_ORDER[:1]:
        g_start(step)

    lax.fori_loop(0, 8, phases, 0)

    def y_wait(s, carry):
        src = (yy + s) & 7
        pltpu.make_async_remote_copy(
            rot, ya.at[src], y_send.at[s], y_recv.at[src],
            device_id=(za, src * 8 + xc), device_id_type=MESH).wait_recv()
        return carry

    lax.fori_loop(1, 8, y_wait, 0)

    def x_copy(s, slot):
        peer = (xx + s) & 3
        return pltpu.make_async_remote_copy(
            ya, xb.at[pl.ds(8 * slot, 8)], x_send.at[s], x_recv.at[slot],
            device_id=(za, yy * 8 + peer * 2 + cc), device_id_type=MESH)

    for s in range(1, 4):
        x_copy(s, xx).start()
    xb[pl.ds(8 * xx, 8)] = ya[...]

    for step in Y_ORDER[1:3]:
        g_start(step)
    lax.fori_loop(8, 20, phases, 0)

    for s in range(1, 4):
        x_copy(s, (xx + s) & 3).wait_recv()

    def z_copy(s, slot):
        return pltpu.make_async_remote_copy(
            xb, zc.at[pl.ds((cc * 8 + slot) * 32, 32)], z_send.at[s], z_recv.at[slot],
            device_id=((za + s) & 7, me), device_id_type=MESH)

    def z_start(s, carry):
        z_copy(s, za).start()
        return carry

    lax.fori_loop(1, KA, z_start, 0)
    zc[pl.ds((cc * 8 + za) * 32, 32)] = xb[...]

    for step in Y_ORDER[3:]:
        g_start(step)
    lax.fori_loop(20, 32, phases, 0)

    def group(step):
        ys = (yy - step) & 7
        arrived = recv1.at[pl.ds(8 * ys, 8)]
        pltpu.make_async_copy(arrived, arrived, g_recv.at[ys]).wait()
        for u in range(8):
            xg[u, 0:ROWS, :] = recv1[ys * 8 + u]
        x = xg[...].reshape(256, COLS)
        x_swapped = swap_parts(x.astype(F32)).astype(BF16)
        lanes = pl.ds(pl.multiple_of(ys * 256, 256), 256)
        total = jnp.dot(cosp[:, lanes], x, preferred_element_type=F32)
        total += jnp.dot(sinp[:, lanes], x_swapped, preferred_element_type=F32)
        if step == 0:
            acc[...] = total
        else:
            acc[...] += total

    @pl.when(working)
    def _():
        for step in Y_ORDER[:5]:
            group(step)

    def z_wait(s, carry):
        z_copy(s, (za + s) & 7).wait_recv()
        return carry

    lax.fori_loop(1, KA, z_wait, 0)

    def c_copy(half):
        part = zc.at[pl.ds(half * 256, 256)]
        return pltpu.make_async_remote_copy(
            part, part, c_send.at[0], c_recv.at[0], device_id=(za, me ^ 1), device_id_type=MESH)

    c_copy(cc).start()

    @pl.when(working)
    def _():
        for step in Y_ORDER[5:]:
            group(step)
        slot = worker_index(me)

        def pack(s, carry):
            d = me ^ s
            rows = acc[pl.ds(pl.multiple_of(8 * d, 8), 8), :]
            send2[d] = jnp.concatenate([rows[:, :128], rows[:, 128:]], axis=0).astype(BF16)

            @pl.when(s > 0)
            def _():
                pltpu.make_async_remote_copy(
                    send2.at[d], blk_out.at[slot], b_send.at[0], b_recv.at[0],
                    device_id=(za, d), device_id_type=MESH).start()

            return carry

        lax.fori_loop(0, PB, pack, 0)
        pltpu.make_async_copy(send2.at[me], blk_out.at[slot], b_recv.at[0]).start()

    c_copy(1 - cc).wait_recv()
    r = iota((1, K), 1)
    place = (((r & 1) * 8 + (r >> 6)) * 4 + ((r >> 1) & 3)) * 8 + ((r >> 3) & 7)
    sub = iota((8, K), 0)
    own = jnp.zeros((8, K), F32)
    other = jnp.zeros((8, K), F32)
    for k in range(8):
        at = jnp.minimum(jnp.sum(jnp.where(home[...] == me * 8 + k, place, 0)), K - 1)
        own = jnp.where(sub == k, zc[at], own)
        at = jnp.minimum(jnp.sum(jnp.where(home[...] == shifted[0, k], place, 0)), K - 1)
        other = jnp.where(sub == k, zc[at], other)
    both = jnp.concatenate([own, other], axis=0)
    for jp in range(32):
        pieces = [both[:, 128 * v : 128 * v + 128] for v in range(4)]
        if jp:
            pieces = [pltpu.roll(piece, 128 - jp, axis=1) for piece in pieces]
        turned = jnp.concatenate(pieces, axis=1)
        upper = turned.astype(BF16)
        lh[16 * jp : 16 * jp + 16, :] = upper
        ll[16 * jp : 16 * jp + 16, :] = (turned - upper.astype(F32)).astype(BF16)
    spread = jnp.where(iota((K, 128), 0) == 32 * (iota((K, 128), 1) // 8), 1.0, 0.0).astype(BF16)
    keep = iota((K, 128), 1) % 8 == iota((K, 128), 0) % 8
    for level, source in ((0, lh), (1, ll)):
        full = jnp.where(keep, jnp.dot(source[...], spread, preferred_element_type=F32), 0.0)
        for jj in range(8):
            for part in range(2):
                a = 16 * (4 * jj + part)
                b = 16 * (4 * jj + 2 + part)
                rows = slice(128 * level + 16 * jj, 128 * level + 16 * jj + 16)
                lanes = slice(128 * part, 128 * part + 128)
                lhs1[rows, lanes] = jnp.concatenate([full[a : a + 8], full[b : b + 8]], axis=0).astype(BF16)
                left = jnp.concatenate([full[a + 8 : a + 16], full[b + 8 : b + 16]], axis=0)
                lhs2[rows, lanes] = (left if part == 0 else -left).astype(BF16)
    outs = [pltpu.make_async_copy(lhs1, lhs1_out, out_sem.at[0]), pltpu.make_async_copy(lhs2, lhs2_out, out_sem.at[1])]
    for out in outs:
        out.start()

    def y_left(s, carry):
        y_copy(s).wait_send()
        return carry

    lax.fori_loop(1, 8, y_left, 0)
    for s in range(1, 4):
        x_copy(s, xx).wait_send()

    def z_left(s, carry):
        z_copy(s, za).wait_send()
        return carry

    lax.fori_loop(1, KA, z_left, 0)
    c_copy(cc).wait_send()

    @pl.when(working)
    def _():
        sent = recv1.at[pl.ds(0, WORKERS - 1)]
        pltpu.make_async_copy(sent, sent, g_send.at[0]).wait()
        sent = send2.at[pl.ds(0, PB - 1)]
        pltpu.make_async_copy(sent, sent, b_send.at[0]).wait()

    @pl.when(jnp.logical_not(working))
    def _():
        sent = recv1.at[pl.ds(0, WORKERS)]
        pltpu.make_async_copy(sent, sent, g_send.at[0]).wait()

    for out in outs:
        out.wait()
    pltpu.make_async_copy(blk_out, blk_out, b_recv.at[0]).wait()


def rotate_kernel(
    blk_hbm, lhs1_hbm, lhs2_hbm, counts_hbm, out, blk, lhs1, lhs2, counts, padded, middle, final, in_sem
):
    reads = [
        pltpu.make_async_copy(source, target, in_sem.at[i])
        for i, (source, target) in enumerate(
            ((blk_hbm, blk), (lhs1_hbm, lhs1), (lhs2_hbm, lhs2), (counts_hbm, counts)))
    ]
    for read in reads:
        read.start()
    lane = iota((8, 128), 1)
    low_half = lane < 64

    def compact_tile(t):
        return blk[t // 2].astype(F32)[8 * (t % 2) : 8 * (t % 2) + 8]

    reads[0].wait()
    tiles = [compact_tile(t) for t in range(108)]

    def turn(x, shift):
        shift %= 128
        return pltpu.roll(x, shift, axis=1) if shift else x

    for n in range(NW):
        for mp in range(8):
            halves = []
            for h in range(2):
                start = VEC * (16 * (2 * mp + h) + n)
                t, off = start // 128, start % 128
                piece = turn(tiles[t], 64 * h - off)
                if off + VEC > 128:
                    spill = turn(tiles[t + 1], 64 * h - off)
                    piece = jnp.where(lane < 128 - off + 64 * h, piece, spill)
                halves.append(piece)
            padded[8 * n : 8 * n + 8, 128 * mp : 128 * mp + 128] = jnp.where(low_half, halves[0], halves[1])

    reads[1].wait()
    for p in range(4):
        lanes = slice(256 * p, 256 * p + 256)
        x = padded[:, lanes]
        rhs = jnp.concatenate([x, swap_parts(x)], axis=0).astype(BF16)
        both = jnp.dot(lhs1[...], rhs, preferred_element_type=F32)
        middle[:, lanes] = both[:128] + both[128:]

    for a in range(8):
        for b in range(8):
            lanes = slice(128 * b, 128 * b + 128)
            first = middle[16 * a : 16 * a + 8, lanes]
            second = middle[16 * a + 8 : 16 * a + 16, lanes]
            place = slice(128 * a, 128 * a + 128)
            padded[16 * b : 16 * b + 8, place] = jnp.where(low_half, first, turn(second, 64))
            padded[16 * b + 8 : 16 * b + 16, place] = jnp.where(low_half, turn(first, 64), second)

    reads[2].wait()
    reads[3].wait()
    sub = iota((8, 1), 0)
    limit = jnp.zeros((8, 1), jnp.int32)
    for k in range(8):
        limit = jnp.where(sub == k, counts[0, k], limit)
    row = iota((128, 256), 0)
    limits = jnp.concatenate([jnp.broadcast_to(limit, (8, 256))] * 16, axis=0)
    for p in range(4):
        lanes = slice(256 * p, 256 * p + 256)
        x = padded[:, lanes]
        x = jnp.concatenate([x, swap_parts(x)], axis=0)
        upper = x.astype(BF16)
        lower = (x - upper.astype(F32)).astype(BF16)
        both = jnp.dot(lhs2[...], upper, preferred_element_type=F32)
        total = both[:128] + (both[128:] + jnp.dot(lhs2[:128, :], lower, preferred_element_type=F32))
        band = jnp.maximum(row // 8, 4 * p + iota((128, 256), 1) // 64)
        final[:, lanes] = jnp.where(band < limits, total, 0.0)

    for t in range(108):
        begin = 128 * t
        value = None
        for q in range(begin // VEC, (begin + 127) // VEC + 1):
            if q >= 256:
                continue
            i, j = q // 16, q % 16
            at = VEC * q - begin
            piece = turn(final[8 * i : 8 * i + 8, 128 * (j // 2) : 128 * (j // 2) + 128], at - 64 * (j % 2))
            value = piece if value is None else jnp.where(lane < at, value, piece)
        out[0, :, begin : begin + 128] = value.astype(BF16)


def per_device(wannier_g, rotations, home_rows, shifted, band_count, lattice):
    vmem = pl.BlockSpec(memory_space=pltpu.VMEM)
    hbm = pl.BlockSpec(memory_space=pltpu.HBM)
    dma = pltpu.SemaphoreType.DMA
    blocks, lhs1, lhs2 = pl.pallas_call(
        comm_kernel,
        out_shape=(
            jax.ShapeDtypeStruct((WORKERS, 16, 128), BF16),
            jax.ShapeDtypeStruct((256, 256), BF16),
            jax.ShapeDtypeStruct((256, 256), BF16),
        ),
        in_specs=[hbm] * 5,
        out_specs=(hbm, hbm, hbm),
        scratch_shapes=[
            pltpu.VMEM((1, K), F32),
            pltpu.VMEM((1, K), jnp.int32),
            pltpu.SMEM((1, 8), jnp.int32),
            pltpu.VMEM((3, 1920), jnp.int32),
            pltpu.VMEM((PB, ROWS, COLS), BF16),
            pltpu.VMEM((8, 32, COLS), BF16),
            pltpu.VMEM((K, COLS), F32),
            pltpu.VMEM((K, 2048), BF16),
            pltpu.VMEM((K, 2048), BF16),
            pltpu.VMEM((PB, 16, 128), BF16),
            pltpu.VMEM((8, 1, 512), F32),
            pltpu.VMEM((32, 1, 512), F32),
            pltpu.VMEM((512, 1, 512), F32),
            pltpu.VMEM((3, 2048), jnp.int32),
            pltpu.VMEM((8, 2048), jnp.int32),
            pltpu.VMEM((K, 512), BF16),
            pltpu.VMEM((K, 512), BF16),
            pltpu.VMEM((256, 256), BF16),
            pltpu.VMEM((256, 256), BF16),
            dma((4,)), dma((1,)), dma((8,)), dma((1,)), dma((1,)),
            dma((8,)), dma((8,)), dma((4,)), dma((4,)), dma((8,)), dma((8,)), dma((1,)), dma((1,)), dma((2,)),
        ],
        compiler_params=pltpu.CompilerParams(
            collective_id=0, has_side_effects=True, vmem_limit_bytes=60 * 1024 * 1024
        ),
        name="exchange",
    )(wannier_g, rotations, home_rows.reshape(1, K), shifted, lattice)
    return pl.pallas_call(
        rotate_kernel,
        out_shape=jax.ShapeDtypeStruct((1, 8, NW * NW * VEC), BF16),
        in_specs=[hbm] * 4,
        out_specs=vmem,
        scratch_shapes=[
            pltpu.VMEM((WORKERS, 16, 128), BF16),
            pltpu.VMEM((256, 256), BF16),
            pltpu.VMEM((256, 256), BF16),
            pltpu.SMEM((1, 8), jnp.int32),
            pltpu.VMEM((128, 1024), F32),
            pltpu.VMEM((128, 1024), F32),
            pltpu.VMEM((128, 1024), F32),
            dma((4,)),
        ],
        compiler_params=pltpu.CompilerParams(vmem_limit_bytes=60 * 1024 * 1024),
        name="rotate",
    )(blocks, lhs1, lhs2, band_count)


def solution(mesh):
    placed = (P("ka", "pb", None), P(("ka", "pb"), None), P(), P("ka", "pb"), P("ka", "pb"), P())
    return jax.shard_map(
        per_device, mesh=mesh, in_specs=placed, out_specs=P("ka", "pb", None), check_vma=False
    )
```

```python
import jax
import jax.numpy as jnp
from jax import lax
from jax.experimental import pallas as pl
from jax.experimental.pallas import tpu as pltpu
from jax.sharding import PartitionSpec as P

NW = 16
NKG = 8
K = 512
VEC = 54
ROWS = 30
PB = 64
KA = 8
Y_ORDER = (1, 7, 2, 6, 3, 5, 4, 0)
EARLY = 4
MIDDLE = 4
WORKERS = 54
COLS = 256
MESH = pl.DeviceIdType.MESH
F32 = jnp.float32
BF16 = jnp.bfloat16
HALF_ROOT = 0.70703125
CUBIC = (0.5 - HALF_ROOT) / 3.0
LINEAR = HALF_ROOT - CUBIC


def worker_index(d):
    return (27 * d + 31) >> 5


def is_worker(d):
    return ((5 * d) & 31) < 27


def iota(shape, axis):
    return lax.broadcasted_iota(jnp.int32, shape, axis)


def swap_parts(x):
    width = x.shape[1]
    even = iota(x.shape, 1) % 2 == 0
    return jnp.where(even, -pltpu.roll(x, width - 1, axis=1), pltpu.roll(x, 1, axis=1))


def wave(t):
    w = (jnp.abs((t & 7) - 4) - 2).astype(F32)
    return w * (LINEAR + CUBIC * (w * w))


def comm_kernel(
    g, rot_hbm, home_hbm, shifted_hbm, lattice_hbm, blk_out, lhs1_out, lhs2_out,
    home, shifted, lattice, recv1, xg, acc, cosp, sinp, send2, ya, xb, zc, lat, third, lh, ll, lhs1, lhs2,
    in_sem, g_send, g_recv, b_send, b_recv, y_send, y_recv, x_send, x_recv, z_send, z_recv, c_send, c_recv, out_sem,
):
    za = lax.axis_index("ka")
    me = lax.axis_index("pb")
    yy = me >> 3
    xc = me & 7
    xx = xc >> 1
    cc = xc & 1
    working = is_worker(me)
    barrier = pltpu.get_barrier_semaphore()
    reads = [
        pltpu.make_async_copy(source, target, in_sem.at[i])
        for i, (source, target) in enumerate(
            ((lattice_hbm, lattice), (rot_hbm, ya.at[yy]), (home_hbm, home), (shifted_hbm, shifted)))
    ]
    for read in reads:
        read.start()

    def greet(s, carry):
        pl.semaphore_signal(barrier, inc=1, device_id=(za, me ^ s), device_id_type=MESH)
        return carry

    lax.fori_loop(1, PB, greet, 0)

    def greet_z(s, carry):
        pl.semaphore_signal(barrier, inc=1, device_id=(za ^ s, me), device_id_type=MESH)
        return carry

    lax.fori_loop(1, KA, greet_z, 0)

    pl.semaphore_wait(barrier, PB - 1 + KA - 1)

    def y_copy(s):
        peer = (yy + s) & 7
        return pltpu.make_async_remote_copy(
            rot_hbm, ya.at[yy], y_send.at[s], y_recv.at[yy],
            device_id=(za, peer * 8 + xc), device_id_type=MESH)

    def y_start(s, carry):
        y_copy(s).start()
        return carry

    lax.fori_loop(1, 8, y_start, 0)

    def g_columns(d):
        return g.at[0, :, pl.ds(pl.multiple_of(worker_index(d) * COLS, COLS), COLS)]

    @pl.when(working)
    def _():
        pltpu.make_async_copy(g_columns(me), recv1.at[me], g_recv.at[yy]).start()

    def g_start(step):
        base = ((yy + step) & 7) * 8

        def one(u, carry):
            d = base + (xc ^ u)

            @pl.when(is_worker(d))
            def _():
                pltpu.make_async_remote_copy(
                    g_columns(d), recv1.at[me], g_send.at[0], g_recv.at[yy],
                    device_id=(za, d), device_id_type=MESH).start()

            return carry

        lax.fori_loop(0 if step else 1, 8, one, 0)

    for step in Y_ORDER[:EARLY]:
        g_start(step)

    def y_wait(s, carry):
        src = (yy + s) & 7
        pltpu.make_async_remote_copy(
            rot_hbm, ya.at[src], y_send.at[s], y_recv.at[src],
            device_id=(za, src * 8 + xc), device_id_type=MESH).wait_recv()
        return carry

    lax.fori_loop(1, 8, y_wait, 0)
    reads[1].wait()

    def x_copy(s, slot):
        peer = (xx + s) & 3
        return pltpu.make_async_remote_copy(
            ya, xb.at[pl.ds(8 * slot, 8)], x_send.at[s], x_recv.at[slot],
            device_id=(za, yy * 8 + peer * 2 + cc), device_id_type=MESH)

    for s in range(1, 4):
        x_copy(s, xx).start()
    for step in Y_ORDER[EARLY:]:
        g_start(step)

    for read in reads[:1] + reads[2:]:
        read.wait()
    xb[pl.ds(8 * xx, 8)] = ya[...]

    lane3 = iota((3, 128), 1)
    for tile in range(16):
        a, off = (120 * tile) // 128, (120 * tile) % 128
        b = min(a + 1, 14)
        first, second = lattice[:, 128 * a : 128 * a + 128], lattice[:, 128 * b : 128 * b + 128]
        out = jnp.zeros((3, 128), jnp.int32)
        for c in range(4):
            shift = (2 * c - off) % 128
            here, there = first, second
            if shift:
                here, there = pltpu.roll(first, shift, axis=1), pltpu.roll(second, shift, axis=1)
            value = jnp.where(lane3 < 128 - off + 2 * c, here, there)
            out = jnp.where(lane3 // 32 == c, value, out)
        lat[:, 128 * tile : 128 * tile + 128] = out
    third[...] = iota((8, 2048), 0) * lat[2:3, :]
    xg[...] = jnp.zeros_like(xg)

    def phases(b, carry):
        first = (b >> 2) * lat[0:1, :]
        second = lat[1:2, :]
        k2 = (b & 3) * 2
        low = (first + k2 * second) + third[...]
        high = (first + (k2 + 1) * second) + third[...]
        t = jnp.concatenate([low, high], axis=0)
        rows = pl.ds(pl.multiple_of(b * 16, 16), 16)
        cosp[rows, :] = wave(t).astype(BF16)
        sinp[rows, :] = wave(t + 6).astype(BF16)
        return carry

    lax.fori_loop(0, 32, phases, 0)

    for s in range(1, 4):
        x_copy(s, (xx + s) & 3).wait_recv()

    def z_copy(s, slot):
        return pltpu.make_async_remote_copy(
            xb, zc.at[pl.ds((cc * 8 + slot) * 32, 32)], z_send.at[s], z_recv.at[slot],
            device_id=((za + s) & 7, me), device_id_type=MESH)

    def z_start(s, carry):
        z_copy(s, za).start()
        return carry

    lax.fori_loop(1, KA, z_start, 0)
    zc[pl.ds((cc * 8 + za) * 32, 32)] = xb[...]

    def group(step):
        ys = (yy - step) & 7
        arrived = recv1.at[pl.ds(8 * ys, 8)]
        pltpu.make_async_copy(arrived, arrived, g_recv.at[ys]).wait()
        for u in range(8):
            xg[u, 0:ROWS, :] = recv1[ys * 8 + u]
        x = xg[...].reshape(256, COLS)
        x_swapped = swap_parts(x.astype(F32)).astype(BF16)
        lanes = pl.ds(pl.multiple_of(ys * 256, 256), 256)
        total = jnp.dot(cosp[:, lanes], x, preferred_element_type=F32)
        total += jnp.dot(sinp[:, lanes], x_swapped, preferred_element_type=F32)
        if step == Y_ORDER[0]:
            acc[...] = total
        else:
            acc[...] += total

    @pl.when(working)
    def _():
        for step in Y_ORDER[:MIDDLE]:
            group(step)

    def z_wait(s, carry):
        z_copy(s, (za + s) & 7).wait_recv()
        return carry

    lax.fori_loop(1, KA, z_wait, 0)

    def c_copy(half):
        part = zc.at[pl.ds(half * 256, 256)]
        return pltpu.make_async_remote_copy(
            part, part, c_send.at[0], c_recv.at[0], device_id=(za, me ^ 1), device_id_type=MESH)

    c_copy(cc).start()

    @pl.when(working)
    def _():
        for step in Y_ORDER[MIDDLE:]:
            group(step)
        slot = worker_index(me)

        def pack(s, carry):
            d = me ^ s
            rows = acc[pl.ds(pl.multiple_of(8 * d, 8), 8), :]
            send2[d] = jnp.concatenate([rows[:, :128], rows[:, 128:]], axis=0).astype(BF16)

            @pl.when(s > 0)
            def _():
                pltpu.make_async_remote_copy(
                    send2.at[d], blk_out.at[slot], b_send.at[0], b_recv.at[0],
                    device_id=(za, d), device_id_type=MESH).start()

            return carry

        lax.fori_loop(0, PB, pack, 0)
        pltpu.make_async_copy(send2.at[me], blk_out.at[slot], b_recv.at[0]).start()

    c_copy(1 - cc).wait_recv()
    r = iota((1, K), 1)
    place = (((r & 1) * 8 + (r >> 6)) * 4 + ((r >> 1) & 3)) * 8 + ((r >> 3) & 7)
    sub = iota((8, K), 0)
    own = jnp.zeros((8, K), F32)
    other = jnp.zeros((8, K), F32)
    for k in range(8):
        at = jnp.minimum(jnp.sum(jnp.where(home[...] == me * 8 + k, place, 0)), K - 1)
        own = jnp.where(sub == k, zc[at], own)
        at = jnp.minimum(jnp.sum(jnp.where(home[...] == shifted[0, k], place, 0)), K - 1)
        other = jnp.where(sub == k, zc[at], other)
    both = jnp.concatenate([own, other], axis=0)
    for jp in range(32):
        pieces = [both[:, 128 * v : 128 * v + 128] for v in range(4)]
        if jp:
            pieces = [pltpu.roll(piece, 128 - jp, axis=1) for piece in pieces]
        turned = jnp.concatenate(pieces, axis=1)
        upper = turned.astype(BF16)
        lh[16 * jp : 16 * jp + 16, :] = upper
        ll[16 * jp : 16 * jp + 16, :] = (turned - upper.astype(F32)).astype(BF16)
    spread = jnp.where(iota((K, 128), 0) == 32 * (iota((K, 128), 1) // 8), 1.0, 0.0).astype(BF16)
    keep = iota((K, 128), 1) % 8 == iota((K, 128), 0) % 8
    for level, source in ((0, lh), (1, ll)):
        full = jnp.where(keep, jnp.dot(source[...], spread, preferred_element_type=F32), 0.0)
        for jj in range(8):
            for part in range(2):
                a = 16 * (4 * jj + part)
                b = 16 * (4 * jj + 2 + part)
                rows = slice(128 * level + 16 * jj, 128 * level + 16 * jj + 16)
                lanes = slice(128 * part, 128 * part + 128)
                lhs1[rows, lanes] = jnp.concatenate([full[a : a + 8], full[b : b + 8]], axis=0).astype(BF16)
                left = jnp.concatenate([full[a + 8 : a + 16], full[b + 8 : b + 16]], axis=0)
                lhs2[rows, lanes] = (left if part == 0 else -left).astype(BF16)
    outs = [pltpu.make_async_copy(lhs1, lhs1_out, out_sem.at[0]), pltpu.make_async_copy(lhs2, lhs2_out, out_sem.at[1])]
    for out in outs:
        out.start()

    def y_left(s, carry):
        y_copy(s).wait_send()
        return carry

    lax.fori_loop(1, 8, y_left, 0)
    for s in range(1, 4):
        x_copy(s, xx).wait_send()

    def z_left(s, carry):
        z_copy(s, za).wait_send()
        return carry

    lax.fori_loop(1, KA, z_left, 0)
    c_copy(cc).wait_send()

    @pl.when(working)
    def _():
        sent = recv1.at[pl.ds(0, WORKERS - 1)]
        pltpu.make_async_copy(sent, sent, g_send.at[0]).wait()
        sent = send2.at[pl.ds(0, PB - 1)]
        pltpu.make_async_copy(sent, sent, b_send.at[0]).wait()

    @pl.when(jnp.logical_not(working))
    def _():
        sent = recv1.at[pl.ds(0, WORKERS)]
        pltpu.make_async_copy(sent, sent, g_send.at[0]).wait()

    for out in outs:
        out.wait()
    pltpu.make_async_copy(blk_out, blk_out, b_recv.at[0]).wait()


def rotate_kernel(
    blk_hbm, lhs1_hbm, lhs2_hbm, counts_hbm, out, blk, lhs1, lhs2, counts, padded, middle, final, in_sem
):
    reads = [
        pltpu.make_async_copy(source, target, in_sem.at[i])
        for i, (source, target) in enumerate(
            ((blk_hbm, blk), (lhs1_hbm, lhs1), (lhs2_hbm, lhs2), (counts_hbm, counts)))
    ]
    for read in reads:
        read.start()
    lane = iota((8, 128), 1)
    low_half = lane < 64

    def compact_tile(t):
        return blk[t // 2].astype(F32)[8 * (t % 2) : 8 * (t % 2) + 8]

    reads[0].wait()
    tiles = [compact_tile(t) for t in range(108)]

    def turn(x, shift):
        shift %= 128
        return pltpu.roll(x, shift, axis=1) if shift else x

    for n in range(NW):
        for mp in range(8):
            halves = []
            for h in range(2):
                start = VEC * (16 * (2 * mp + h) + n)
                t, off = start // 128, start % 128
                piece = turn(tiles[t], 64 * h - off)
                if off + VEC > 128:
                    spill = turn(tiles[t + 1], 64 * h - off)
                    piece = jnp.where(lane < 128 - off + 64 * h, piece, spill)
                halves.append(piece)
            padded[8 * n : 8 * n + 8, 128 * mp : 128 * mp + 128] = jnp.where(low_half, halves[0], halves[1])

    reads[1].wait()
    for p in range(4):
        lanes = slice(256 * p, 256 * p + 256)
        x = padded[:, lanes]
        rhs = jnp.concatenate([x, swap_parts(x)], axis=0).astype(BF16)
        both = jnp.dot(lhs1[...], rhs, preferred_element_type=F32)
        middle[:, lanes] = both[:128] + both[128:]

    for a in range(8):
        for b in range(8):
            lanes = slice(128 * b, 128 * b + 128)
            first = middle[16 * a : 16 * a + 8, lanes]
            second = middle[16 * a + 8 : 16 * a + 16, lanes]
            place = slice(128 * a, 128 * a + 128)
            padded[16 * b : 16 * b + 8, place] = jnp.where(low_half, first, turn(second, 64))
            padded[16 * b + 8 : 16 * b + 16, place] = jnp.where(low_half, turn(first, 64), second)

    reads[2].wait()
    reads[3].wait()
    sub = iota((8, 1), 0)
    limit = jnp.zeros((8, 1), jnp.int32)
    for k in range(8):
        limit = jnp.where(sub == k, counts[0, k], limit)
    row = iota((128, 256), 0)
    limits = jnp.concatenate([jnp.broadcast_to(limit, (8, 256))] * 16, axis=0)
    for p in range(4):
        lanes = slice(256 * p, 256 * p + 256)
        x = padded[:, lanes]
        x = jnp.concatenate([x, swap_parts(x)], axis=0)
        upper = x.astype(BF16)
        lower = (x - upper.astype(F32)).astype(BF16)
        both = jnp.dot(lhs2[...], upper, preferred_element_type=F32)
        total = both[:128] + (both[128:] + jnp.dot(lhs2[:128, :], lower, preferred_element_type=F32))
        band = jnp.maximum(row // 8, 4 * p + iota((128, 256), 1) // 64)
        final[:, lanes] = jnp.where(band < limits, total, 0.0)

    for t in range(108):
        begin = 128 * t
        value = None
        for q in range(begin // VEC, (begin + 127) // VEC + 1):
            if q >= 256:
                continue
            i, j = q // 16, q % 16
            at = VEC * q - begin
            piece = turn(final[8 * i : 8 * i + 8, 128 * (j // 2) : 128 * (j // 2) + 128], at - 64 * (j % 2))
            value = piece if value is None else jnp.where(lane < at, value, piece)
        out[0, :, begin : begin + 128] = value.astype(BF16)


def per_device(wannier_g, rotations, home_rows, shifted, band_count, lattice):
    vmem = pl.BlockSpec(memory_space=pltpu.VMEM)
    hbm = pl.BlockSpec(memory_space=pltpu.HBM)
    dma = pltpu.SemaphoreType.DMA
    blocks, lhs1, lhs2 = pl.pallas_call(
        comm_kernel,
        out_shape=(
            jax.ShapeDtypeStruct((WORKERS, 16, 128), BF16),
            jax.ShapeDtypeStruct((256, 256), BF16),
            jax.ShapeDtypeStruct((256, 256), BF16),
        ),
        in_specs=[hbm] * 5,
        out_specs=(hbm, hbm, hbm),
        scratch_shapes=[
            pltpu.VMEM((1, K), jnp.int32),
            pltpu.SMEM((1, 8), jnp.int32),
            pltpu.VMEM((3, 1920), jnp.int32),
            pltpu.VMEM((PB, ROWS, COLS), BF16),
            pltpu.VMEM((8, 32, COLS), BF16),
            pltpu.VMEM((K, COLS), F32),
            pltpu.VMEM((K, 2048), BF16),
            pltpu.VMEM((K, 2048), BF16),
            pltpu.VMEM((PB, 16, 128), BF16),
            pltpu.VMEM((8, 1, 512), F32),
            pltpu.VMEM((32, 1, 512), F32),
            pltpu.VMEM((512, 1, 512), F32),
            pltpu.VMEM((3, 2048), jnp.int32),
            pltpu.VMEM((8, 2048), jnp.int32),
            pltpu.VMEM((K, 512), BF16),
            pltpu.VMEM((K, 512), BF16),
            pltpu.VMEM((256, 256), BF16),
            pltpu.VMEM((256, 256), BF16),
            dma((4,)), dma((1,)), dma((8,)), dma((1,)), dma((1,)),
            dma((8,)), dma((8,)), dma((4,)), dma((4,)), dma((8,)), dma((8,)), dma((1,)), dma((1,)), dma((2,)),
        ],
        compiler_params=pltpu.CompilerParams(
            collective_id=0, has_side_effects=True, vmem_limit_bytes=60 * 1024 * 1024
        ),
        name="exchange",
    )(wannier_g, rotations, home_rows.reshape(1, K), shifted, lattice)
    return pl.pallas_call(
        rotate_kernel,
        out_shape=jax.ShapeDtypeStruct((1, 8, NW * NW * VEC), BF16),
        in_specs=[hbm] * 4,
        out_specs=vmem,
        scratch_shapes=[
            pltpu.VMEM((WORKERS, 16, 128), BF16),
            pltpu.VMEM((256, 256), BF16),
            pltpu.VMEM((256, 256), BF16),
            pltpu.SMEM((1, 8), jnp.int32),
            pltpu.VMEM((128, 1024), F32),
            pltpu.VMEM((128, 1024), F32),
            pltpu.VMEM((128, 1024), F32),
            dma((4,)),
        ],
        compiler_params=pltpu.CompilerParams(vmem_limit_bytes=60 * 1024 * 1024),
        name="rotate",
    )(blocks, lhs1, lhs2, band_count)


def solution(mesh):
    placed = (P("ka", "pb", None), P(("ka", "pb"), None), P(), P("ka", "pb"), P("ka", "pb"), P())
    return jax.shard_map(
        per_device, mesh=mesh, in_specs=placed, out_specs=P("ka", "pb", None), check_vma=False
    )
```

```python
import jax
import jax.numpy as jnp
from jax import lax
from jax.experimental import pallas as pl
from jax.experimental.pallas import tpu as pltpu
from jax.sharding import PartitionSpec as P

NW = 16
NKG = 8
K = 512
VEC = 54
ROWS = 30
PB = 64
KA = 8
Y_ORDER = (1, 7, 2, 6, 3, 5, 4, 0)
B_ORDER = (4, 3, 5, 2, 6, 1, 7, 0)
EARLY = 3
MIDDLE = 6
WORKERS = 54
COLS = 256
MESH = pl.DeviceIdType.MESH
F32 = jnp.float32
BF16 = jnp.bfloat16
HALF_ROOT = 0.70703125
CUBIC = (0.5 - HALF_ROOT) / 3.0
LINEAR = HALF_ROOT - CUBIC


def worker_index(d):
    return (27 * d + 31) >> 5


def is_worker(d):
    return ((5 * d) & 31) < 27


def iota(shape, axis):
    return lax.broadcasted_iota(jnp.int32, shape, axis)


def swap_parts(x):
    width = x.shape[1]
    even = iota(x.shape, 1) % 2 == 0
    return jnp.where(even, -pltpu.roll(x, width - 1, axis=1), pltpu.roll(x, 1, axis=1))


def wave(t):
    w = (jnp.abs((t & 7) - 4) - 2).astype(F32)
    return w * (LINEAR + CUBIC * (w * w))


def comm_kernel(
    g, rot_hbm, home_hbm, shifted_hbm, lattice_hbm, blk_out, lhs1_out, lhs2_out,
    home, shifted, lattice, recv1, xg, acc, table, send2, ya, xb, zc, lat, third, lh, lhs1, lhs2,
    in_sem, g_send, g_recv, b_send, b_recv, y_send, y_recv, x_send, x_recv, z_send, z_recv, c_send, c_recv, out_sem, above,
):
    za = lax.axis_index("ka")
    me = lax.axis_index("pb")
    yy = me >> 3
    xc = me & 7
    xx = xc >> 1
    cc = xc & 1
    working = is_worker(me)
    barrier = pltpu.get_barrier_semaphore()
    reads = [
        pltpu.make_async_copy(source, target, in_sem.at[i])
        for i, (source, target) in enumerate(
            ((lattice_hbm, lattice), (rot_hbm, ya.at[yy]), (home_hbm, home), (shifted_hbm, shifted)))
    ]
    for read in reads:
        read.start()

    def greet(s, carry):
        pl.semaphore_signal(barrier, inc=1, device_id=(za, me ^ s), device_id_type=MESH)
        return carry

    lax.fori_loop(1, PB, greet, 0)

    def greet_z(s, carry):
        pl.semaphore_signal(barrier, inc=1, device_id=(za + s, me), device_id_type=MESH)
        return carry

    lax.fori_loop(1, KA - za, greet_z, 0)

    pl.semaphore_wait(barrier, PB - 1 + za)

    def y_copy(s):
        peer = (yy + s) & 7
        return pltpu.make_async_remote_copy(
            rot_hbm, ya.at[yy], y_send.at[s], y_recv.at[yy],
            device_id=(za, peer * 8 + xc), device_id_type=MESH)

    def y_start(s, carry):
        y_copy(s).start()
        return carry

    lax.fori_loop(1, 8, y_start, 0)

    def g_columns(d):
        return g.at[0, :, pl.ds(pl.multiple_of(worker_index(d) * COLS, COLS), COLS)]

    @pl.when(working)
    def _():
        pltpu.make_async_copy(g_columns(me), recv1.at[me], g_recv.at[yy]).start()

    def g_start(step):
        base = ((yy + step) & 7) * 8

        def one(u, carry):
            d = base + (xc ^ u)

            @pl.when(is_worker(d))
            def _():
                pltpu.make_async_remote_copy(
                    g_columns(d), recv1.at[me], g_send.at[0], g_recv.at[yy],
                    device_id=(za, d), device_id_type=MESH).start()

            return carry

        lax.fori_loop(0 if step else 1, 8, one, 0)

    for step in Y_ORDER[:EARLY]:
        g_start(step)

    def y_wait(s, carry):
        src = (yy + s) & 7
        pltpu.make_async_remote_copy(
            rot_hbm, ya.at[src], y_send.at[s], y_recv.at[src],
            device_id=(za, src * 8 + xc), device_id_type=MESH).wait_recv()
        return carry

    lax.fori_loop(1, 8, y_wait, 0)
    reads[1].wait()

    line = jnp.concatenate([ya[y] for y in range(8)], axis=0)
    xb[xx] = jnp.concatenate([line[:, :256], line[:, 256:]], axis=0).astype(BF16)

    def x_copy(s, slot):
        peer = (xx + s) & 3
        return pltpu.make_async_remote_copy(
            xb.at[xx], xb.at[slot], x_send.at[s], x_recv.at[slot],
            device_id=(za, yy * 8 + peer * 2 + cc), device_id_type=MESH)

    for s in range(1, 4):
        x_copy(s, xx).start()
    for step in Y_ORDER[EARLY:]:
        g_start(step)

    def greet_lower(s, carry):
        pl.semaphore_signal(above, inc=1, device_id=(za - s, me), device_id_type=MESH)
        return carry

    lax.fori_loop(1, za + 1, greet_lower, 0)

    for read in reads[:1] + reads[2:]:
        read.wait()

    lane3 = iota((3, 128), 1)
    for tile in range(16):
        a, off = (120 * tile) // 128, (120 * tile) % 128
        b = min(a + 1, 14)
        first, second = lattice[:, 128 * a : 128 * a + 128], lattice[:, 128 * b : 128 * b + 128]
        out = jnp.zeros((3, 128), jnp.int32)
        for c in range(4):
            shift = (2 * c - off) % 128
            here, there = first, second
            if shift:
                here, there = pltpu.roll(first, shift, axis=1), pltpu.roll(second, shift, axis=1)
            value = jnp.where(lane3 < 128 - off + 2 * c, here, there)
            out = jnp.where(lane3 // 32 == c, value, out)
        lat[:, 128 * tile : 128 * tile + 128] = out
    third[...] = iota((8, 2048), 0) * lat[2:3, :]
    xg[...] = jnp.zeros_like(xg)

    def phases(b, carry):
        first = (b >> 2) * lat[0:1, :]
        second = lat[1:2, :]
        k2 = (b & 3) * 2
        low = (first + k2 * second) + third[...]
        high = (first + (k2 + 1) * second) + third[...]
        t = jnp.concatenate([low, high], axis=0)
        rows = pl.ds(pl.multiple_of(b * 16, 16), 16)
        cosines = wave(t).astype(BF16)
        sines = wave(t + 6).astype(BF16)
        for ys in range(8):
            lanes = slice(256 * ys, 256 * ys + 256)
            table[rows, 512 * ys : 512 * ys + 256] = cosines[:, lanes]
            table[rows, 512 * ys + 256 : 512 * ys + 512] = sines[:, lanes]
        return carry

    lax.fori_loop(0, 32, phases, 0)

    for s in range(1, 4):
        x_copy(s, (xx + s) & 3).wait_recv()

    def z_copy(s, slot):
        return pltpu.make_async_remote_copy(
            xb, zc.at[pl.ds((cc * 8 + slot) * 4, 4)], z_send.at[s], z_recv.at[slot],
            device_id=((za + s) & 7, me), device_id_type=MESH)

    def z_start(s, carry):
        z_copy(s, za).start()
        return carry

    @pl.when(za < KA - 1)
    def _():
        pl.semaphore_wait(above, KA - 1 - za)

    lax.fori_loop(1, KA, z_start, 0)
    zc[pl.ds((cc * 8 + za) * 4, 4)] = xb[...]

    def group(step):
        ys = (yy - step) & 7
        arrived = recv1.at[pl.ds(8 * ys, 8)]
        pltpu.make_async_copy(arrived, arrived, g_recv.at[ys]).wait()
        for u in range(8):
            xg[u, 0:ROWS, :] = recv1[ys * 8 + u]
        x = xg[...].reshape(256, COLS)
        x_swapped = swap_parts(x.astype(F32)).astype(BF16)
        lanes = pl.ds(pl.multiple_of(ys * 512, 512), 512)
        total = jnp.dot(
            table[:, lanes], jnp.concatenate([x, x_swapped], axis=0), preferred_element_type=F32)
        if step == Y_ORDER[0]:
            acc[...] = total
        else:
            acc[...] += total

    @pl.when(working)
    def _():
        for step in Y_ORDER[:MIDDLE]:
            group(step)

    def z_wait(s, carry):
        z_copy(s, (za + s) & 7).wait_recv()
        return carry

    lax.fori_loop(1, KA, z_wait, 0)

    def c_copy(half):
        part = zc.at[pl.ds(half * 32, 32)]
        return pltpu.make_async_remote_copy(
            part, part, c_send.at[0], c_recv.at[0], device_id=(za, me ^ 1), device_id_type=MESH)

    c_copy(cc).start()

    @pl.when(working)
    def _():
        for step in Y_ORDER[MIDDLE:]:
            group(step)
        slot = worker_index(me)

        for step in B_ORDER:
            base = ((yy + step) & 7) * 8
            rows = acc[pl.ds(pl.multiple_of(base * 8, 64), 64), :]
            for u in range(8):
                part = rows[8 * u : 8 * u + 8]
                send2[base + u] = jnp.concatenate([part[:, :128], part[:, 128:]], axis=0).astype(BF16)

            def one(u, carry):
                d = base + (xc ^ u)
                pltpu.make_async_remote_copy(
                    send2.at[d], blk_out.at[slot], b_send.at[0], b_recv.at[0],
                    device_id=(za, d), device_id_type=MESH).start()
                return carry

            lax.fori_loop(0 if step else 1, 8, one, 0)
        pltpu.make_async_copy(send2.at[me], blk_out.at[slot], b_recv.at[0]).start()

    c_copy(1 - cc).wait_recv()
    r = iota((1, K), 1)
    place = (((r & 1) * 8 + (r >> 6)) * 4 + ((r >> 1) & 3)) * 8 + ((r >> 3) & 7)
    sub = iota((8, K), 0)
    sub8 = iota((8, 256), 0)

    def pick(point):
        at = jnp.minimum(jnp.sum(jnp.where(home[...] == point, place, 0)), K - 1)
        block = zc[at >> 3].astype(F32)
        here = sub8 == (at & 7)
        halves = [
            jnp.sum(jnp.where(here, block[8 * h : 8 * h + 8], 0.0), axis=0, keepdims=True) for h in range(2)
        ]
        return jnp.concatenate(halves, axis=1)

    own = jnp.zeros((8, K), F32)
    other = jnp.zeros((8, K), F32)
    for k in range(8):
        own = jnp.where(sub == k, pick(me * 8 + k), own)
        other = jnp.where(sub == k, pick(shifted[0, k]), other)
    both = jnp.concatenate([own, other], axis=0)
    for jp in range(32):
        pieces = [both[:, 128 * v : 128 * v + 128] for v in range(4)]
        if jp:
            pieces = [pltpu.roll(piece, 128 - jp, axis=1) for piece in pieces]
        lh[16 * jp : 16 * jp + 16, :] = jnp.concatenate(pieces, axis=1).astype(BF16)
    spread = jnp.where(iota((K, 128), 0) == 32 * (iota((K, 128), 1) // 8), 1.0, 0.0).astype(BF16)
    keep = iota((K, 128), 1) % 8 == iota((K, 128), 0) % 8
    full = jnp.where(keep, jnp.dot(lh[...], spread, preferred_element_type=F32), 0.0)
    for jj in range(8):
        for part in range(2):
            a = 16 * (4 * jj + part)
            b = 16 * (4 * jj + 2 + part)
            rows = slice(16 * jj, 16 * jj + 16)
            lanes = slice(128 * part, 128 * part + 128)
            lhs1[rows, lanes] = jnp.concatenate([full[a : a + 8], full[b : b + 8]], axis=0).astype(BF16)
            left = jnp.concatenate([full[a + 8 : a + 16], full[b + 8 : b + 16]], axis=0)
            lhs2[rows, lanes] = (left if part == 0 else -left).astype(BF16)
    outs = [pltpu.make_async_copy(lhs1, lhs1_out, out_sem.at[0]), pltpu.make_async_copy(lhs2, lhs2_out, out_sem.at[1])]
    for out in outs:
        out.start()

    def y_left(s, carry):
        y_copy(s).wait_send()
        return carry

    lax.fori_loop(1, 8, y_left, 0)
    for s in range(1, 4):
        x_copy(s, xx).wait_send()

    def z_left(s, carry):
        z_copy(s, za).wait_send()
        return carry

    lax.fori_loop(1, KA, z_left, 0)
    c_copy(cc).wait_send()

    @pl.when(working)
    def _():
        sent = recv1.at[pl.ds(0, WORKERS - 1)]
        pltpu.make_async_copy(sent, sent, g_send.at[0]).wait()
        sent = send2.at[pl.ds(0, PB - 1)]
        pltpu.make_async_copy(sent, sent, b_send.at[0]).wait()

    @pl.when(jnp.logical_not(working))
    def _():
        sent = recv1.at[pl.ds(0, WORKERS)]
        pltpu.make_async_copy(sent, sent, g_send.at[0]).wait()

    for out in outs:
        out.wait()
    pltpu.make_async_copy(blk_out, blk_out, b_recv.at[0]).wait()


def rotate_kernel(
    blk_hbm, lhs1_hbm, lhs2_hbm, counts_hbm, out, blk, lhs1, lhs2, counts, padded, middle, final, in_sem
):
    reads = [
        pltpu.make_async_copy(source, target, in_sem.at[i])
        for i, (source, target) in enumerate(
            ((blk_hbm, blk), (lhs1_hbm, lhs1), (lhs2_hbm, lhs2), (counts_hbm, counts)))
    ]
    for read in reads:
        read.start()
    lane = iota((8, 128), 1)
    low_half = lane < 64

    def compact_tile(t):
        return blk[t // 2].astype(F32)[8 * (t % 2) : 8 * (t % 2) + 8]

    reads[0].wait()
    tiles = [compact_tile(t) for t in range(108)]

    def turn(x, shift):
        shift %= 128
        return pltpu.roll(x, shift, axis=1) if shift else x

    for n in range(NW):
        for mp in range(8):
            halves = []
            for h in range(2):
                start = VEC * (16 * (2 * mp + h) + n)
                t, off = start // 128, start % 128
                piece = turn(tiles[t], 64 * h - off)
                if off + VEC > 128:
                    spill = turn(tiles[t + 1], 64 * h - off)
                    piece = jnp.where(lane < 128 - off + 64 * h, piece, spill)
                halves.append(piece)
            padded[8 * n : 8 * n + 8, 128 * mp : 128 * mp + 128] = jnp.where(low_half, halves[0], halves[1])

    reads[1].wait()
    for p in range(4):
        lanes = slice(256 * p, 256 * p + 256)
        x = padded[:, lanes]
        rhs = jnp.concatenate([x, swap_parts(x)], axis=0).astype(BF16)
        middle[:, lanes] = jnp.dot(lhs1[...], rhs, preferred_element_type=F32)

    for a in range(8):
        for b in range(8):
            lanes = slice(128 * b, 128 * b + 128)
            first = middle[16 * a : 16 * a + 8, lanes]
            second = middle[16 * a + 8 : 16 * a + 16, lanes]
            place = slice(128 * a, 128 * a + 128)
            padded[16 * b : 16 * b + 8, place] = jnp.where(low_half, first, turn(second, 64))
            padded[16 * b + 8 : 16 * b + 16, place] = jnp.where(low_half, turn(first, 64), second)

    reads[2].wait()
    reads[3].wait()
    sub = iota((8, 1), 0)
    limit = jnp.zeros((8, 1), jnp.int32)
    for k in range(8):
        limit = jnp.where(sub == k, counts[0, k], limit)
    row = iota((128, 256), 0)
    limits = jnp.concatenate([jnp.broadcast_to(limit, (8, 256))] * 16, axis=0)
    for p in range(4):
        lanes = slice(256 * p, 256 * p + 256)
        x = padded[:, lanes]
        x = jnp.concatenate([x, swap_parts(x)], axis=0)
        upper = x.astype(BF16)
        lower = (x - upper.astype(F32)).astype(BF16)
        total = jnp.dot(lhs2[...], upper, preferred_element_type=F32)
        total += jnp.dot(lhs2[...], lower, preferred_element_type=F32)
        band = jnp.maximum(row // 8, 4 * p + iota((128, 256), 1) // 64)
        final[:, lanes] = jnp.where(band < limits, total, 0.0)

    for t in range(108):
        begin = 128 * t
        value = None
        for q in range(begin // VEC, (begin + 127) // VEC + 1):
            if q >= 256:
                continue
            i, j = q // 16, q % 16
            at = VEC * q - begin
            piece = turn(final[8 * i : 8 * i + 8, 128 * (j // 2) : 128 * (j // 2) + 128], at - 64 * (j % 2))
            value = piece if value is None else jnp.where(lane < at, value, piece)
        out[0, :, begin : begin + 128] = value.astype(BF16)


def per_device(wannier_g, rotations, home_rows, shifted, band_count, lattice):
    vmem = pl.BlockSpec(memory_space=pltpu.VMEM)
    hbm = pl.BlockSpec(memory_space=pltpu.HBM)
    dma = pltpu.SemaphoreType.DMA
    blocks, lhs1, lhs2 = pl.pallas_call(
        comm_kernel,
        out_shape=(
            jax.ShapeDtypeStruct((WORKERS, 16, 128), BF16),
            jax.ShapeDtypeStruct((128, 256), BF16),
            jax.ShapeDtypeStruct((128, 256), BF16),
        ),
        in_specs=[hbm] * 5,
        out_specs=(hbm, hbm, hbm),
        scratch_shapes=[
            pltpu.VMEM((1, K), jnp.int32),
            pltpu.SMEM((1, 8), jnp.int32),
            pltpu.VMEM((3, 1920), jnp.int32),
            pltpu.VMEM((PB, ROWS, COLS), BF16),
            pltpu.VMEM((8, 32, COLS), BF16),
            pltpu.VMEM((K, COLS), F32),
            pltpu.VMEM((K, 4096), BF16),
            pltpu.VMEM((PB, 16, 128), BF16),
            pltpu.VMEM((8, 1, 512), F32),
            pltpu.VMEM((4, 16, 256), BF16),
            pltpu.VMEM((64, 16, 256), BF16),
            pltpu.VMEM((3, 2048), jnp.int32),
            pltpu.VMEM((8, 2048), jnp.int32),
            pltpu.VMEM((K, 512), BF16),
            pltpu.VMEM((128, 256), BF16),
            pltpu.VMEM((128, 256), BF16),
            dma((4,)), dma((1,)), dma((8,)), dma((1,)), dma((1,)),
            dma((8,)), dma((8,)), dma((4,)), dma((4,)), dma((8,)), dma((8,)), dma((1,)), dma((1,)), dma((2,)),
            pltpu.SemaphoreType.REGULAR,
        ],
        compiler_params=pltpu.CompilerParams(
            collective_id=0, has_side_effects=True, vmem_limit_bytes=60 * 1024 * 1024
        ),
        name="exchange",
    )(wannier_g, rotations, home_rows.reshape(1, K), shifted, lattice)
    return pl.pallas_call(
        rotate_kernel,
        out_shape=jax.ShapeDtypeStruct((1, 8, NW * NW * VEC), BF16),
        in_specs=[hbm] * 4,
        out_specs=vmem,
        scratch_shapes=[
            pltpu.VMEM((WORKERS, 16, 128), BF16),
            pltpu.VMEM((128, 256), BF16),
            pltpu.VMEM((128, 256), BF16),
            pltpu.SMEM((1, 8), jnp.int32),
            pltpu.VMEM((128, 1024), F32),
            pltpu.VMEM((128, 1024), F32),
            pltpu.VMEM((128, 1024), F32),
            dma((4,)),
        ],
        compiler_params=pltpu.CompilerParams(vmem_limit_bytes=60 * 1024 * 1024),
        name="rotate",
    )(blocks, lhs1, lhs2, band_count)


def solution(mesh):
    placed = (P("ka", "pb", None), P(("ka", "pb"), None), P(), P("ka", "pb"), P("ka", "pb"), P())
    return jax.shard_map(
        per_device, mesh=mesh, in_specs=placed, out_specs=P("ka", "pb", None), check_vma=False
    )
```

```python
import jax
import jax.numpy as jnp
from jax import lax
from jax.experimental import pallas as pl
from jax.experimental.pallas import tpu as pltpu
from jax.sharding import PartitionSpec as P

NW = 16
NKG = 8
K = 512
VEC = 54
ROWS = 30
PB = 64
KA = 8
Y_ORDER = (1, 7, 2, 6, 3, 5, 4, 0)
B_ORDER = (4, 3, 5, 2, 6, 1, 7, 0)
EARLY = 4
MIDDLE = 8
WORKERS = 54
COLS = 256
MESH = pl.DeviceIdType.MESH
F32 = jnp.float32
BF16 = jnp.bfloat16
HALF_ROOT = 0.70703125
CUBIC = (0.5 - HALF_ROOT) / 3.0
LINEAR = HALF_ROOT - CUBIC


def worker_index(d):
    return (27 * d + 31) >> 5


def is_worker(d):
    return ((5 * d) & 31) < 27


def iota(shape, axis):
    return lax.broadcasted_iota(jnp.int32, shape, axis)


def swap_parts(x):
    width = x.shape[1]
    even = iota(x.shape, 1) % 2 == 0
    return jnp.where(even, -pltpu.roll(x, width - 1, axis=1), pltpu.roll(x, 1, axis=1))


def wave(t):
    w = (jnp.abs((t & 7) - 4) - 2).astype(F32)
    return w * (LINEAR + CUBIC * (w * w))


def comm_kernel(
    g, rot_hbm, home_hbm, shifted_hbm, lattice_hbm, blk_out, lhs1_out, lhs2_out,
    gv, home, shifted, lattice, recv1, xg, acc, table, send2, ya, xb, zc, lat, third, lh, lhs1, lhs2,
    in_sem, g_send, g_recv, b_send, b_recv, y_send, y_recv, x_send, x_recv, z_send, z_recv, c_send, c_recv, out_sem, above,
):
    za = lax.axis_index("ka")
    me = lax.axis_index("pb")
    yy = me >> 3
    xc = me & 7
    xx = xc >> 1
    cc = xc & 1
    working = is_worker(me)
    barrier = pltpu.get_barrier_semaphore()
    reads = [
        pltpu.make_async_copy(source, target, in_sem.at[i])
        for i, (source, target) in enumerate(
            ((lattice_hbm, lattice), (rot_hbm, ya.at[yy]), (home_hbm, home), (shifted_hbm, shifted)))
    ]
    fetch = pltpu.make_async_copy(g.at[0], gv, in_sem.at[4])
    fetch.start()
    for read in reads:
        read.start()

    def greet(s, carry):
        pl.semaphore_signal(barrier, inc=1, device_id=(za, me ^ s), device_id_type=MESH)
        return carry

    lax.fori_loop(1, PB, greet, 0)

    def greet_z(s, carry):
        pl.semaphore_signal(barrier, inc=1, device_id=(za + s, me), device_id_type=MESH)
        return carry

    lax.fori_loop(1, KA - za, greet_z, 0)

    fetch.wait()
    pl.semaphore_wait(barrier, PB - 1 + za)

    def y_copy(s):
        peer = (yy + s) & 7
        return pltpu.make_async_remote_copy(
            rot_hbm, ya.at[yy], y_send.at[s], y_recv.at[yy],
            device_id=(za, peer * 8 + xc), device_id_type=MESH)

    def y_start(s, carry):
        y_copy(s).start()
        return carry

    lax.fori_loop(1, 8, y_start, 0)

    def g_columns(d):
        return gv.at[:, pl.ds(pl.multiple_of(worker_index(d) * COLS, COLS), COLS)]

    @pl.when(working)
    def _():
        pltpu.make_async_copy(g_columns(me), recv1.at[me], g_recv.at[yy]).start()

    def g_start(step):
        base = ((yy + step) & 7) * 8

        def one(u, carry):
            d = base + (xc ^ u)

            @pl.when(is_worker(d))
            def _():
                pltpu.make_async_remote_copy(
                    g_columns(d), recv1.at[me], g_send.at[0], g_recv.at[yy],
                    device_id=(za, d), device_id_type=MESH).start()

            return carry

        lax.fori_loop(0 if step else 1, 8, one, 0)

    for step in Y_ORDER[:EARLY]:
        g_start(step)

    def y_wait(s, carry):
        src = (yy + s) & 7
        pltpu.make_async_remote_copy(
            rot_hbm, ya.at[src], y_send.at[s], y_recv.at[src],
            device_id=(za, src * 8 + xc), device_id_type=MESH).wait_recv()
        return carry

    lax.fori_loop(1, 8, y_wait, 0)
    reads[1].wait()

    line = jnp.concatenate([ya[y] for y in range(8)], axis=0)
    xb[xx] = jnp.concatenate([line[:, :256], line[:, 256:]], axis=0).astype(BF16)

    def x_copy(s, slot):
        peer = (xx + s) & 3
        return pltpu.make_async_remote_copy(
            xb.at[xx], xb.at[slot], x_send.at[s], x_recv.at[slot],
            device_id=(za, yy * 8 + peer * 2 + cc), device_id_type=MESH)

    for s in range(1, 4):
        x_copy(s, xx).start()
    for step in Y_ORDER[EARLY:]:
        g_start(step)

    def greet_lower(s, carry):
        pl.semaphore_signal(above, inc=1, device_id=(za - s, me), device_id_type=MESH)
        return carry

    lax.fori_loop(1, za + 1, greet_lower, 0)

    for read in reads[:1] + reads[2:]:
        read.wait()

    lane3 = iota((3, 128), 1)
    for tile in range(16):
        a, off = (120 * tile) // 128, (120 * tile) % 128
        b = min(a + 1, 14)
        first, second = lattice[:, 128 * a : 128 * a + 128], lattice[:, 128 * b : 128 * b + 128]
        out = jnp.zeros((3, 128), jnp.int32)
        for c in range(4):
            shift = (2 * c - off) % 128
            here, there = first, second
            if shift:
                here, there = pltpu.roll(first, shift, axis=1), pltpu.roll(second, shift, axis=1)
            value = jnp.where(lane3 < 128 - off + 2 * c, here, there)
            out = jnp.where(lane3 // 32 == c, value, out)
        lat[:, 128 * tile : 128 * tile + 128] = out
    third[...] = iota((8, 2048), 0) * lat[2:3, :]
    xg[...] = jnp.zeros_like(xg)

    def phases(b, carry):
        first = (b >> 2) * lat[0:1, :]
        second = lat[1:2, :]
        k2 = (b & 3) * 2
        low = (first + k2 * second) + third[...]
        high = (first + (k2 + 1) * second) + third[...]
        t = jnp.concatenate([low, high], axis=0)
        rows = pl.ds(pl.multiple_of(b * 16, 16), 16)
        cosines = wave(t).astype(BF16)
        sines = wave(t + 6).astype(BF16)
        for ys in range(8):
            lanes = slice(256 * ys, 256 * ys + 256)
            table[rows, 512 * ys : 512 * ys + 256] = cosines[:, lanes]
            table[rows, 512 * ys + 256 : 512 * ys + 512] = sines[:, lanes]
        return carry

    lax.fori_loop(0, 32, phases, 0)

    for s in range(1, 4):
        x_copy(s, (xx + s) & 3).wait_recv()

    def z_copy(s, slot):
        return pltpu.make_async_remote_copy(
            xb, zc.at[pl.ds((cc * 8 + slot) * 4, 4)], z_send.at[s], z_recv.at[slot],
            device_id=((za + s) & 7, me), device_id_type=MESH)

    def z_start(s, carry):
        z_copy(s, za).start()
        return carry

    @pl.when(za < KA - 1)
    def _():
        pl.semaphore_wait(above, KA - 1 - za)

    lax.fori_loop(1, KA, z_start, 0)
    zc[pl.ds((cc * 8 + za) * 4, 4)] = xb[...]

    def group(step):
        ys = (yy - step) & 7
        arrived = recv1.at[pl.ds(8 * ys, 8)]
        pltpu.make_async_copy(arrived, arrived, g_recv.at[ys]).wait()
        for u in range(8):
            xg[u, 0:ROWS, :] = recv1[ys * 8 + u]
        x = xg[...].reshape(256, COLS)
        x_swapped = swap_parts(x.astype(F32)).astype(BF16)
        lanes = pl.ds(pl.multiple_of(ys * 512, 512), 512)
        total = jnp.dot(
            table[:, lanes], jnp.concatenate([x, x_swapped], axis=0), preferred_element_type=F32)
        if step == Y_ORDER[0]:
            acc[...] = total
        else:
            acc[...] += total

    @pl.when(working)
    def _():
        for step in Y_ORDER[:MIDDLE]:
            group(step)

    def z_wait(s, carry):
        z_copy(s, (za + s) & 7).wait_recv()
        return carry

    lax.fori_loop(1, KA, z_wait, 0)

    def c_copy(half):
        part = zc.at[pl.ds(half * 32, 32)]
        return pltpu.make_async_remote_copy(
            part, part, c_send.at[0], c_recv.at[0], device_id=(za, me ^ 1), device_id_type=MESH)

    c_copy(cc).start()

    @pl.when(working)
    def _():
        for step in Y_ORDER[MIDDLE:]:
            group(step)
        slot = worker_index(me)

        for step in B_ORDER:
            base = ((yy + step) & 7) * 8
            rows = acc[pl.ds(pl.multiple_of(base * 8, 64), 64), :]
            for u in range(8):
                part = rows[8 * u : 8 * u + 8]
                send2[base + u] = jnp.concatenate([part[:, :128], part[:, 128:]], axis=0).astype(BF16)

            def one(u, carry):
                d = base + (xc ^ u)
                pltpu.make_async_remote_copy(
                    send2.at[d], blk_out.at[slot], b_send.at[0], b_recv.at[0],
                    device_id=(za, d), device_id_type=MESH).start()
                return carry

            lax.fori_loop(0 if step else 1, 8, one, 0)
        pltpu.make_async_copy(send2.at[me], blk_out.at[slot], b_recv.at[0]).start()

    c_copy(1 - cc).wait_recv()
    r = iota((1, K), 1)
    place = (((r & 1) * 8 + (r >> 6)) * 4 + ((r >> 1) & 3)) * 8 + ((r >> 3) & 7)
    sub = iota((8, K), 0)
    sub8 = iota((8, 256), 0)

    def pick(point):
        at = jnp.minimum(jnp.sum(jnp.where(home[...] == point, place, 0)), K - 1)
        block = zc[at >> 3].astype(F32)
        here = sub8 == (at & 7)
        halves = [
            jnp.sum(jnp.where(here, block[8 * h : 8 * h + 8], 0.0), axis=0, keepdims=True) for h in range(2)
        ]
        return jnp.concatenate(halves, axis=1)

    own = jnp.zeros((8, K), F32)
    other = jnp.zeros((8, K), F32)
    for k in range(8):
        own = jnp.where(sub == k, pick(me * 8 + k), own)
        other = jnp.where(sub == k, pick(shifted[0, k]), other)
    both = jnp.concatenate([own, other], axis=0)
    for jp in range(32):
        pieces = [both[:, 128 * v : 128 * v + 128] for v in range(4)]
        if jp:
            pieces = [pltpu.roll(piece, 128 - jp, axis=1) for piece in pieces]
        lh[16 * jp : 16 * jp + 16, :] = jnp.concatenate(pieces, axis=1).astype(BF16)
    spread = jnp.where(iota((K, 128), 0) == 32 * (iota((K, 128), 1) // 8), 1.0, 0.0).astype(BF16)
    keep = iota((K, 128), 1) % 8 == iota((K, 128), 0) % 8
    full = jnp.where(keep, jnp.dot(lh[...], spread, preferred_element_type=F32), 0.0)
    for jj in range(8):
        for part in range(2):
            a = 16 * (4 * jj + part)
            b = 16 * (4 * jj + 2 + part)
            rows = slice(16 * jj, 16 * jj + 16)
            lanes = slice(128 * part, 128 * part + 128)
            lhs1[rows, lanes] = jnp.concatenate([full[a : a + 8], full[b : b + 8]], axis=0).astype(BF16)
            left = jnp.concatenate([full[a + 8 : a + 16], full[b + 8 : b + 16]], axis=0)
            lhs2[rows, lanes] = (left if part == 0 else -left).astype(BF16)
    outs = [pltpu.make_async_copy(lhs1, lhs1_out, out_sem.at[0]), pltpu.make_async_copy(lhs2, lhs2_out, out_sem.at[1])]
    for out in outs:
        out.start()

    def y_left(s, carry):
        y_copy(s).wait_send()
        return carry

    lax.fori_loop(1, 8, y_left, 0)
    for s in range(1, 4):
        x_copy(s, xx).wait_send()

    def z_left(s, carry):
        z_copy(s, za).wait_send()
        return carry

    lax.fori_loop(1, KA, z_left, 0)
    c_copy(cc).wait_send()

    @pl.when(working)
    def _():
        sent = recv1.at[pl.ds(0, WORKERS - 1)]
        pltpu.make_async_copy(sent, sent, g_send.at[0]).wait()
        sent = send2.at[pl.ds(0, PB - 1)]
        pltpu.make_async_copy(sent, sent, b_send.at[0]).wait()

    @pl.when(jnp.logical_not(working))
    def _():
        sent = recv1.at[pl.ds(0, WORKERS)]
        pltpu.make_async_copy(sent, sent, g_send.at[0]).wait()

    for out in outs:
        out.wait()
    pltpu.make_async_copy(blk_out, blk_out, b_recv.at[0]).wait()


def rotate_kernel(
    blk_hbm, lhs1_hbm, lhs2_hbm, counts_hbm, out, blk, lhs1, lhs2, counts, padded, middle, final, in_sem
):
    reads = [
        pltpu.make_async_copy(source, target, in_sem.at[i])
        for i, (source, target) in enumerate(
            ((blk_hbm, blk), (lhs1_hbm, lhs1), (lhs2_hbm, lhs2), (counts_hbm, counts)))
    ]
    for read in reads:
        read.start()
    lane = iota((8, 128), 1)
    low_half = lane < 64

    def compact_tile(t):
        return blk[t // 2].astype(F32)[8 * (t % 2) : 8 * (t % 2) + 8]

    reads[0].wait()
    tiles = [compact_tile(t) for t in range(108)]

    def turn(x, shift):
        shift %= 128
        return pltpu.roll(x, shift, axis=1) if shift else x

    for n in range(NW):
        for mp in range(8):
            halves = []
            for h in range(2):
                start = VEC * (16 * (2 * mp + h) + n)
                t, off = start // 128, start % 128
                piece = turn(tiles[t], 64 * h - off)
                if off + VEC > 128:
                    spill = turn(tiles[t + 1], 64 * h - off)
                    piece = jnp.where(lane < 128 - off + 64 * h, piece, spill)
                halves.append(piece)
            padded[8 * n : 8 * n + 8, 128 * mp : 128 * mp + 128] = jnp.where(low_half, halves[0], halves[1])

    reads[1].wait()
    for p in range(4):
        lanes = slice(256 * p, 256 * p + 256)
        x = padded[:, lanes]
        rhs = jnp.concatenate([x, swap_parts(x)], axis=0).astype(BF16)
        middle[:, lanes] = jnp.dot(lhs1[...], rhs, preferred_element_type=F32)

    for a in range(8):
        for b in range(8):
            lanes = slice(128 * b, 128 * b + 128)
            first = middle[16 * a : 16 * a + 8, lanes]
            second = middle[16 * a + 8 : 16 * a + 16, lanes]
            place = slice(128 * a, 128 * a + 128)
            padded[16 * b : 16 * b + 8, place] = jnp.where(low_half, first, turn(second, 64))
            padded[16 * b + 8 : 16 * b + 16, place] = jnp.where(low_half, turn(first, 64), second)

    reads[2].wait()
    reads[3].wait()
    sub = iota((8, 1), 0)
    limit = jnp.zeros((8, 1), jnp.int32)
    for k in range(8):
        limit = jnp.where(sub == k, counts[0, k], limit)
    row = iota((128, 256), 0)
    limits = jnp.concatenate([jnp.broadcast_to(limit, (8, 256))] * 16, axis=0)
    for p in range(4):
        lanes = slice(256 * p, 256 * p + 256)
        x = padded[:, lanes]
        x = jnp.concatenate([x, swap_parts(x)], axis=0)
        upper = x.astype(BF16)
        lower = (x - upper.astype(F32)).astype(BF16)
        total = jnp.dot(lhs2[...], upper, preferred_element_type=F32)
        total += jnp.dot(lhs2[...], lower, preferred_element_type=F32)
        band = jnp.maximum(row // 8, 4 * p + iota((128, 256), 1) // 64)
        final[:, lanes] = jnp.where(band < limits, total, 0.0)

    for t in range(108):
        begin = 128 * t
        value = None
        for q in range(begin // VEC, (begin + 127) // VEC + 1):
            if q >= 256:
                continue
            i, j = q // 16, q % 16
            at = VEC * q - begin
            piece = turn(final[8 * i : 8 * i + 8, 128 * (j // 2) : 128 * (j // 2) + 128], at - 64 * (j % 2))
            value = piece if value is None else jnp.where(lane < at, value, piece)
        out[0, :, begin : begin + 128] = value.astype(BF16)


def per_device(wannier_g, rotations, home_rows, shifted, band_count, lattice):
    vmem = pl.BlockSpec(memory_space=pltpu.VMEM)
    hbm = pl.BlockSpec(memory_space=pltpu.HBM)
    dma = pltpu.SemaphoreType.DMA
    blocks, lhs1, lhs2 = pl.pallas_call(
        comm_kernel,
        out_shape=(
            jax.ShapeDtypeStruct((WORKERS, 16, 128), BF16),
            jax.ShapeDtypeStruct((128, 256), BF16),
            jax.ShapeDtypeStruct((128, 256), BF16),
        ),
        in_specs=[hbm] * 5,
        out_specs=(hbm, hbm, hbm),
        scratch_shapes=[
            pltpu.VMEM((ROWS, NW * NW * VEC), BF16),
            pltpu.VMEM((1, K), jnp.int32),
            pltpu.SMEM((1, 8), jnp.int32),
            pltpu.VMEM((3, 1920), jnp.int32),
            pltpu.VMEM((PB, ROWS, COLS), BF16),
            pltpu.VMEM((8, 32, COLS), BF16),
            pltpu.VMEM((K, COLS), F32),
            pltpu.VMEM((K, 4096), BF16),
            pltpu.VMEM((PB, 16, 128), BF16),
            pltpu.VMEM((8, 1, 512), F32),
            pltpu.VMEM((4, 16, 256), BF16),
            pltpu.VMEM((64, 16, 256), BF16),
            pltpu.VMEM((3, 2048), jnp.int32),
            pltpu.VMEM((8, 2048), jnp.int32),
            pltpu.VMEM((K, 512), BF16),
            pltpu.VMEM((128, 256), BF16),
            pltpu.VMEM((128, 256), BF16),
            dma((5,)), dma((1,)), dma((8,)), dma((1,)), dma((1,)),
            dma((8,)), dma((8,)), dma((4,)), dma((4,)), dma((8,)), dma((8,)), dma((1,)), dma((1,)), dma((2,)),
            pltpu.SemaphoreType.REGULAR,
        ],
        compiler_params=pltpu.CompilerParams(
            collective_id=0, has_side_effects=True, vmem_limit_bytes=60 * 1024 * 1024
        ),
        name="exchange",
    )(wannier_g, rotations, home_rows.reshape(1, K), shifted, lattice)
    return pl.pallas_call(
        rotate_kernel,
        out_shape=jax.ShapeDtypeStruct((1, 8, NW * NW * VEC), BF16),
        in_specs=[hbm] * 4,
        out_specs=vmem,
        scratch_shapes=[
            pltpu.VMEM((WORKERS, 16, 128), BF16),
            pltpu.VMEM((128, 256), BF16),
            pltpu.VMEM((128, 256), BF16),
            pltpu.SMEM((1, 8), jnp.int32),
            pltpu.VMEM((128, 1024), F32),
            pltpu.VMEM((128, 1024), F32),
            pltpu.VMEM((128, 1024), F32),
            dma((4,)),
        ],
        compiler_params=pltpu.CompilerParams(vmem_limit_bytes=60 * 1024 * 1024),
        name="rotate",
    )(blocks, lhs1, lhs2, band_count)


def solution(mesh):
    placed = (P("ka", "pb", None), P(("ka", "pb"), None), P(), P("ka", "pb"), P("ka", "pb"), P())
    return jax.shard_map(
        per_device, mesh=mesh, in_specs=placed, out_specs=P("ka", "pb", None), check_vma=False
    )
```

```python
import jax
import jax.numpy as jnp
from jax import lax
from jax.experimental import pallas as pl
from jax.experimental.pallas import tpu as pltpu
from jax.sharding import PartitionSpec as P

NW = 16
NKG = 8
K = 512
VEC = 54
ROWS = 30
PB = 64
KA = 8
Y_ORDER = (2, 6, 3, 5, 1, 7, 4, 0)
B_ORDER = (4, 3, 5, 2, 6, 1, 7, 0)
EARLY = 4
WORKERS = 54
COLS = 256
MESH = pl.DeviceIdType.MESH
F32 = jnp.float32
BF16 = jnp.bfloat16
HALF_ROOT = 0.70703125
CUBIC = (0.5 - HALF_ROOT) / 3.0
LINEAR = HALF_ROOT - CUBIC


def worker_index(d):
    return (27 * d + 31) >> 5


def is_worker(d):
    return ((5 * d) & 31) < 27


def iota(shape, axis):
    return lax.broadcasted_iota(jnp.int32, shape, axis)


def swap_parts(x):
    width = x.shape[1]
    even = iota(x.shape, 1) % 2 == 0
    return jnp.where(even, -pltpu.roll(x, width - 1, axis=1), pltpu.roll(x, 1, axis=1))


def wave(t):
    w = (jnp.abs((t & 7) - 4) - 2).astype(F32)
    return w * (LINEAR + CUBIC * (w * w))


def comm_kernel(
    g, rot_hbm, home_hbm, shifted_hbm, lattice_hbm, blk_out, lhs1_out, lhs2_out,
    gv, home, shifted, lattice, recv1, xg, acc, table, send2, ya, xb, zc, lat, third, lh, lhs1, lhs2, mate, give, take,
    in_sem, g_send, g_recv, b_send, b_recv, y_send, y_recv, x_send, x_recv, z_send, z_recv, c_send, c_recv, out_sem, above,
):
    za = lax.axis_index("ka")
    me = lax.axis_index("pb")
    yy = me >> 3
    xc = me & 7
    xx = xc >> 1
    cc = xc & 1
    working = is_worker(me)
    barrier = pltpu.get_barrier_semaphore()
    reads = [
        pltpu.make_async_copy(source, target, in_sem.at[i])
        for i, (source, target) in enumerate(
            ((lattice_hbm, lattice), (rot_hbm, ya.at[yy]), (home_hbm, home), (shifted_hbm, shifted)))
    ]
    fetch = pltpu.make_async_copy(g.at[0], gv, in_sem.at[4])
    fetch.start()
    for read in reads:
        read.start()

    def greet(s, carry):
        pl.semaphore_signal(barrier, inc=1, device_id=(za, me ^ s), device_id_type=MESH)
        return carry

    lax.fori_loop(1, PB, greet, 0)

    def greet_z(s, carry):
        pl.semaphore_signal(barrier, inc=1, device_id=(za + s, me), device_id_type=MESH)
        return carry

    lax.fori_loop(1, KA - za, greet_z, 0)

    fetch.wait()
    pl.semaphore_wait(barrier, PB - 1 + za)

    def y_copy(s):
        peer = (yy + s) & 7
        return pltpu.make_async_remote_copy(
            rot_hbm, ya.at[yy], y_send.at[s], y_recv.at[yy],
            device_id=(za, peer * 8 + xc), device_id_type=MESH)

    def y_start(s, carry):
        y_copy(s).start()
        return carry

    lax.fori_loop(1, 8, y_start, 0)

    def mate_copy():
        return pltpu.make_async_remote_copy(
            shifted_hbm, mate, c_send.at[1], c_recv.at[1], device_id=(za, me ^ 1), device_id_type=MESH)

    mate_copy().start()

    def g_columns(d):
        return gv.at[:, pl.ds(pl.multiple_of(worker_index(d) * COLS, COLS), COLS)]

    @pl.when(working)
    def _():
        pltpu.make_async_copy(g_columns(me), recv1.at[me], g_recv.at[yy]).start()

    def g_start(step):
        base = ((yy + step) & 7) * 8

        def one(u, carry):
            d = base + (xc ^ u)

            @pl.when(is_worker(d))
            def _():
                pltpu.make_async_remote_copy(
                    g_columns(d), recv1.at[me], g_send.at[0], g_recv.at[yy],
                    device_id=(za, d), device_id_type=MESH).start()

            return carry

        lax.fori_loop(0 if step else 1, 8, one, 0)

    for step in Y_ORDER[:EARLY]:
        g_start(step)

    def y_wait(s, carry):
        src = (yy + s) & 7
        pltpu.make_async_remote_copy(
            rot_hbm, ya.at[src], y_send.at[s], y_recv.at[src],
            device_id=(za, src * 8 + xc), device_id_type=MESH).wait_recv()
        return carry

    lax.fori_loop(1, 8, y_wait, 0)
    reads[1].wait()

    line = jnp.concatenate([ya[y] for y in range(8)], axis=0)
    xb[xx] = jnp.concatenate([line[:, :256], line[:, 256:]], axis=0).astype(BF16)

    def x_copy(s, slot):
        peer = (xx + s) & 3
        return pltpu.make_async_remote_copy(
            xb.at[xx], xb.at[slot], x_send.at[s], x_recv.at[slot],
            device_id=(za, yy * 8 + peer * 2 + cc), device_id_type=MESH)

    for s in range(1, 4):
        x_copy(s, xx).start()
    for step in Y_ORDER[EARLY:]:
        g_start(step)

    def greet_lower(s, carry):
        pl.semaphore_signal(above, inc=1, device_id=(za - s, me), device_id_type=MESH)
        return carry

    lax.fori_loop(1, za + 1, greet_lower, 0)

    for read in reads[:1] + reads[2:]:
        read.wait()

    lane3 = iota((3, 128), 1)
    for tile in range(16):
        a, off = (120 * tile) // 128, (120 * tile) % 128
        b = min(a + 1, 14)
        first, second = lattice[:, 128 * a : 128 * a + 128], lattice[:, 128 * b : 128 * b + 128]
        out = jnp.zeros((3, 128), jnp.int32)
        for c in range(4):
            shift = (2 * c - off) % 128
            here, there = first, second
            if shift:
                here, there = pltpu.roll(first, shift, axis=1), pltpu.roll(second, shift, axis=1)
            value = jnp.where(lane3 < 128 - off + 2 * c, here, there)
            out = jnp.where(lane3 // 32 == c, value, out)
        lat[:, 128 * tile : 128 * tile + 128] = out
    third[...] = iota((8, 2048), 0) * lat[2:3, :]
    xg[...] = jnp.zeros_like(xg)

    def phases(b, carry):
        first = (b >> 2) * lat[0:1, :]
        second = lat[1:2, :]
        k2 = (b & 3) * 2
        low = (first + k2 * second) + third[...]
        high = (first + (k2 + 1) * second) + third[...]
        t = jnp.concatenate([low, high], axis=0)
        rows = pl.ds(pl.multiple_of(b * 16, 16), 16)
        cosines = wave(t).astype(BF16)
        sines = wave(t + 6).astype(BF16)
        for ys in range(8):
            lanes = slice(256 * ys, 256 * ys + 256)
            table[rows, 512 * ys : 512 * ys + 256] = cosines[:, lanes]
            table[rows, 512 * ys + 256 : 512 * ys + 512] = sines[:, lanes]
        return carry

    lax.fori_loop(0, 32, phases, 0)

    for s in range(1, 4):
        x_copy(s, (xx + s) & 3).wait_recv()

    def z_copy(s, slot):
        return pltpu.make_async_remote_copy(
            xb, zc.at[pl.ds(slot * 4, 4)], z_send.at[s], z_recv.at[slot],
            device_id=((za + s) & 7, me), device_id_type=MESH)

    def z_start(s, carry):
        z_copy(s, za).start()
        return carry

    @pl.when(za < KA - 1)
    def _():
        pl.semaphore_wait(above, KA - 1 - za)

    lax.fori_loop(1, KA, z_start, 0)
    zc[pl.ds(za * 4, 4)] = xb[...]

    def group(step):
        ys = (yy - step) & 7
        arrived = recv1.at[pl.ds(8 * ys, 8)]
        pltpu.make_async_copy(arrived, arrived, g_recv.at[ys]).wait()
        for u in range(8):
            xg[u, 0:ROWS, :] = recv1[ys * 8 + u]
        x = xg[...].reshape(256, COLS)
        x_swapped = swap_parts(x.astype(F32)).astype(BF16)
        lanes = pl.ds(pl.multiple_of(ys * 512, 512), 512)
        total = jnp.dot(
            table[:, lanes], jnp.concatenate([x, x_swapped], axis=0), preferred_element_type=F32)
        if step == Y_ORDER[0]:
            acc[...] = total
        else:
            acc[...] += total

    @pl.when(working)
    def _():
        for step in Y_ORDER:
            group(step)
        slot = worker_index(me)

        for step in B_ORDER:
            base = ((yy + step) & 7) * 8
            rows = acc[pl.ds(pl.multiple_of(base * 8, 64), 64), :]
            for u in range(8):
                part = rows[8 * u : 8 * u + 8]
                send2[base + u] = jnp.concatenate([part[:, :128], part[:, 128:]], axis=0).astype(BF16)

            def one(u, carry):
                d = base + (xc ^ u)
                pltpu.make_async_remote_copy(
                    send2.at[d], blk_out.at[slot], b_send.at[0], b_recv.at[0],
                    device_id=(za, d), device_id_type=MESH).start()
                return carry

            lax.fori_loop(0 if step else 1, 8, one, 0)
        pltpu.make_async_copy(send2.at[me], blk_out.at[slot], b_recv.at[0]).start()

    def z_wait(s, carry):
        z_copy(s, (za + s) & 7).wait_recv()
        return carry

    lax.fori_loop(1, KA, z_wait, 0)
    mate_copy().wait_recv()
    r = iota((1, K), 1)
    place = (((r & 1) * 8 + (r >> 6)) * 4 + ((r >> 1) & 3)) * 8 + ((r >> 3) & 7)
    sub = iota((8, K), 0)
    sub8 = iota((8, 256), 0)

    def pick(point):
        at = jnp.minimum(jnp.sum(jnp.where(home[...] == point, place, 0)), K - 1)
        block = zc[(at >> 3) & 31].astype(F32)
        here = sub8 == (at & 7) + 8 * ((at >> 8) ^ cc)
        halves = [
            jnp.sum(jnp.where(here, block[8 * h : 8 * h + 8], 0.0), axis=0, keepdims=True) for h in range(2)
        ]
        return jnp.concatenate(halves, axis=1)

    def picked(first, moved):
        own = jnp.zeros((8, K), F32)
        other = jnp.zeros((8, K), F32)
        for k in range(8):
            own = jnp.where(sub == k, pick(first + k), own)
            other = jnp.where(sub == k, pick(moved[:, k : k + 1]), other)
        return jnp.concatenate([own, other], axis=0)

    give[...] = picked((me ^ 1) * 8, mate[...])

    def c_copy():
        return pltpu.make_async_remote_copy(
            give, take, c_send.at[0], c_recv.at[0], device_id=(za, me ^ 1), device_id_type=MESH)

    c_copy().start()
    both = picked(me * 8, shifted[...])
    c_copy().wait_recv()
    both += take[...]
    for jp in range(32):
        pieces = [both[:, 128 * v : 128 * v + 128] for v in range(4)]
        if jp:
            pieces = [pltpu.roll(piece, 128 - jp, axis=1) for piece in pieces]
        lh[16 * jp : 16 * jp + 16, :] = jnp.concatenate(pieces, axis=1).astype(BF16)
    spread = jnp.where(iota((K, 128), 0) == 32 * (iota((K, 128), 1) // 8), 1.0, 0.0).astype(BF16)
    keep = iota((K, 128), 1) % 8 == iota((K, 128), 0) % 8
    full = jnp.where(keep, jnp.dot(lh[...], spread, preferred_element_type=F32), 0.0)
    for jj in range(8):
        for part in range(2):
            a = 16 * (4 * jj + part)
            b = 16 * (4 * jj + 2 + part)
            rows = slice(16 * jj, 16 * jj + 16)
            lanes = slice(128 * part, 128 * part + 128)
            lhs1[rows, lanes] = jnp.concatenate([full[a : a + 8], full[b : b + 8]], axis=0).astype(BF16)
            left = jnp.concatenate([full[a + 8 : a + 16], full[b + 8 : b + 16]], axis=0)
            lhs2[rows, lanes] = (left if part == 0 else -left).astype(BF16)
    outs = [pltpu.make_async_copy(lhs1, lhs1_out, out_sem.at[0]), pltpu.make_async_copy(lhs2, lhs2_out, out_sem.at[1])]
    for out in outs:
        out.start()

    def y_left(s, carry):
        y_copy(s).wait_send()
        return carry

    lax.fori_loop(1, 8, y_left, 0)
    for s in range(1, 4):
        x_copy(s, xx).wait_send()

    def z_left(s, carry):
        z_copy(s, za).wait_send()
        return carry

    lax.fori_loop(1, KA, z_left, 0)
    c_copy().wait_send()
    mate_copy().wait_send()

    @pl.when(working)
    def _():
        sent = recv1.at[pl.ds(0, WORKERS - 1)]
        pltpu.make_async_copy(sent, sent, g_send.at[0]).wait()
        sent = send2.at[pl.ds(0, PB - 1)]
        pltpu.make_async_copy(sent, sent, b_send.at[0]).wait()

    @pl.when(jnp.logical_not(working))
    def _():
        sent = recv1.at[pl.ds(0, WORKERS)]
        pltpu.make_async_copy(sent, sent, g_send.at[0]).wait()

    for out in outs:
        out.wait()
    pltpu.make_async_copy(blk_out, blk_out, b_recv.at[0]).wait()


def rotate_kernel(
    blk_hbm, lhs1_hbm, lhs2_hbm, counts_hbm, out, blk, lhs1, lhs2, counts, padded, middle, final, in_sem
):
    reads = [
        pltpu.make_async_copy(source, target, in_sem.at[i])
        for i, (source, target) in enumerate(
            ((blk_hbm, blk), (lhs1_hbm, lhs1), (lhs2_hbm, lhs2), (counts_hbm, counts)))
    ]
    for read in reads:
        read.start()
    lane = iota((8, 128), 1)
    low_half = lane < 64

    def compact_tile(t):
        return blk[t // 2].astype(F32)[8 * (t % 2) : 8 * (t % 2) + 8]

    reads[0].wait()
    tiles = [compact_tile(t) for t in range(108)]

    def turn(x, shift):
        shift %= 128
        return pltpu.roll(x, shift, axis=1) if shift else x

    for n in range(NW):
        for mp in range(8):
            halves = []
            for h in range(2):
                start = VEC * (16 * (2 * mp + h) + n)
                t, off = start // 128, start % 128
                piece = turn(tiles[t], 64 * h - off)
                if off + VEC > 128:
                    spill = turn(tiles[t + 1], 64 * h - off)
                    piece = jnp.where(lane < 128 - off + 64 * h, piece, spill)
                halves.append(piece)
            padded[8 * n : 8 * n + 8, 128 * mp : 128 * mp + 128] = jnp.where(low_half, halves[0], halves[1])

    reads[1].wait()
    for p in range(4):
        lanes = slice(256 * p, 256 * p + 256)
        x = padded[:, lanes]
        rhs = jnp.concatenate([x, swap_parts(x)], axis=0).astype(BF16)
        middle[:, lanes] = jnp.dot(lhs1[...], rhs, preferred_element_type=F32)

    for a in range(8):
        for b in range(8):
            lanes = slice(128 * b, 128 * b + 128)
            first = middle[16 * a : 16 * a + 8, lanes]
            second = middle[16 * a + 8 : 16 * a + 16, lanes]
            place = slice(128 * a, 128 * a + 128)
            padded[16 * b : 16 * b + 8, place] = jnp.where(low_half, first, turn(second, 64))
            padded[16 * b + 8 : 16 * b + 16, place] = jnp.where(low_half, turn(first, 64), second)

    reads[2].wait()
    reads[3].wait()
    sub = iota((8, 1), 0)
    limit = jnp.zeros((8, 1), jnp.int32)
    for k in range(8):
        limit = jnp.where(sub == k, counts[0, k], limit)
    row = iota((128, 256), 0)
    limits = jnp.concatenate([jnp.broadcast_to(limit, (8, 256))] * 16, axis=0)
    for p in range(4):
        lanes = slice(256 * p, 256 * p + 256)
        x = padded[:, lanes]
        x = jnp.concatenate([x, swap_parts(x)], axis=0)
        upper = x.astype(BF16)
        lower = (x - upper.astype(F32)).astype(BF16)
        total = jnp.dot(lhs2[...], upper, preferred_element_type=F32)
        total += jnp.dot(lhs2[...], lower, preferred_element_type=F32)
        band = jnp.maximum(row // 8, 4 * p + iota((128, 256), 1) // 64)
        final[:, lanes] = jnp.where(band < limits, total, 0.0)

    for t in range(108):
        begin = 128 * t
        value = None
        for q in range(begin // VEC, (begin + 127) // VEC + 1):
            if q >= 256:
                continue
            i, j = q // 16, q % 16
            at = VEC * q - begin
            piece = turn(final[8 * i : 8 * i + 8, 128 * (j // 2) : 128 * (j // 2) + 128], at - 64 * (j % 2))
            value = piece if value is None else jnp.where(lane < at, value, piece)
        out[0, :, begin : begin + 128] = value.astype(BF16)


def per_device(wannier_g, rotations, home_rows, shifted, band_count, lattice):
    vmem = pl.BlockSpec(memory_space=pltpu.VMEM)
    hbm = pl.BlockSpec(memory_space=pltpu.HBM)
    dma = pltpu.SemaphoreType.DMA
    blocks, lhs1, lhs2 = pl.pallas_call(
        comm_kernel,
        out_shape=(
            jax.ShapeDtypeStruct((WORKERS, 16, 128), BF16),
            jax.ShapeDtypeStruct((128, 256), BF16),
            jax.ShapeDtypeStruct((128, 256), BF16),
        ),
        in_specs=[hbm] * 5,
        out_specs=(hbm, hbm, hbm),
        scratch_shapes=[
            pltpu.VMEM((ROWS, NW * NW * VEC), BF16),
            pltpu.VMEM((1, K), jnp.int32),
            pltpu.VMEM((1, 8), jnp.int32),
            pltpu.VMEM((3, 1920), jnp.int32),
            pltpu.VMEM((PB, ROWS, COLS), BF16),
            pltpu.VMEM((8, 32, COLS), BF16),
            pltpu.VMEM((K, COLS), F32),
            pltpu.VMEM((K, 4096), BF16),
            pltpu.VMEM((PB, 16, 128), BF16),
            pltpu.VMEM((8, 1, 512), F32),
            pltpu.VMEM((4, 16, 256), BF16),
            pltpu.VMEM((32, 16, 256), BF16),
            pltpu.VMEM((3, 2048), jnp.int32),
            pltpu.VMEM((8, 2048), jnp.int32),
            pltpu.VMEM((K, 512), BF16),
            pltpu.VMEM((128, 256), BF16),
            pltpu.VMEM((128, 256), BF16),
            pltpu.VMEM((1, 8), jnp.int32),
            pltpu.VMEM((16, K), F32),
            pltpu.VMEM((16, K), F32),
            dma((5,)), dma((1,)), dma((8,)), dma((1,)), dma((1,)),
            dma((8,)), dma((8,)), dma((4,)), dma((4,)), dma((8,)), dma((8,)), dma((2,)), dma((2,)), dma((2,)),
            pltpu.SemaphoreType.REGULAR,
        ],
        compiler_params=pltpu.CompilerParams(
            collective_id=0, has_side_effects=True, vmem_limit_bytes=60 * 1024 * 1024
        ),
        name="exchange",
    )(wannier_g, rotations, home_rows.reshape(1, K), shifted, lattice)
    return pl.pallas_call(
        rotate_kernel,
        out_shape=jax.ShapeDtypeStruct((1, 8, NW * NW * VEC), BF16),
        in_specs=[hbm] * 4,
        out_specs=vmem,
        scratch_shapes=[
            pltpu.VMEM((WORKERS, 16, 128), BF16),
            pltpu.VMEM((128, 256), BF16),
            pltpu.VMEM((128, 256), BF16),
            pltpu.SMEM((1, 8), jnp.int32),
            pltpu.VMEM((128, 1024), F32),
            pltpu.VMEM((128, 1024), F32),
            pltpu.VMEM((128, 1024), F32),
            dma((4,)),
        ],
        compiler_params=pltpu.CompilerParams(vmem_limit_bytes=60 * 1024 * 1024),
        name="rotate",
    )(blocks, lhs1, lhs2, band_count)


def solution(mesh):
    placed = (P("ka", "pb", None), P(("ka", "pb"), None), P(), P("ka", "pb"), P("ka", "pb"), P())
    return jax.shard_map(
        per_device, mesh=mesh, in_specs=placed, out_specs=P("ka", "pb", None), check_vma=False
    )
```

```python
import jax
import jax.numpy as jnp
from jax import lax
from jax.experimental import pallas as pl
from jax.experimental.pallas import tpu as pltpu
from jax.sharding import PartitionSpec as P

NW = 16
NKG = 8
K = 512
VEC = 54
ROWS = 30
PB = 64
KA = 8
Y_ORDER = (2, 6, 3, 5, 1, 7, 4, 0)
B_ORDER = (4, 3, 5, 2, 6, 1, 7, 0)
EARLY = 4
WORKERS = 54
COLS = 256
MESH = pl.DeviceIdType.MESH
F32 = jnp.float32
BF16 = jnp.bfloat16
HALF_ROOT = 0.70703125
CUBIC = (0.5 - HALF_ROOT) / 3.0
LINEAR = HALF_ROOT - CUBIC


def worker_index(d):
    return (27 * d + 31) >> 5


def is_worker(d):
    return ((5 * d) & 31) < 27


def iota(shape, axis):
    return lax.broadcasted_iota(jnp.int32, shape, axis)


def swap_parts(x):
    width = x.shape[1]
    even = iota(x.shape, 1) % 2 == 0
    return jnp.where(even, -pltpu.roll(x, width - 1, axis=1), pltpu.roll(x, 1, axis=1))


def wave(t):
    w = (jnp.abs((t & 7) - 4) - 2).astype(F32)
    return w * (LINEAR + CUBIC * (w * w))


def comm_kernel(
    g, rot_hbm, home_hbm, shifted_hbm, lattice_hbm, blk_out, lhs1_out, lhs2_out,
    gv, home, shifted, lattice, recv1, xg, acc, table, send2, ya, xb, zc, lat, third, lh, lhs1, lhs2, mate, give, take,
    in_sem, g_send, g_recv, b_send, b_recv, y_send, y_recv, x_send, x_recv, z_send, z_recv, c_send, c_recv, out_sem, above,
):
    za = lax.axis_index("ka")
    me = lax.axis_index("pb")
    yy = me >> 3
    xc = me & 7
    xx = xc >> 1
    cc = xc & 1
    working = is_worker(me)
    barrier = pltpu.get_barrier_semaphore()
    reads = [
        pltpu.make_async_copy(source, target, in_sem.at[i])
        for i, (source, target) in enumerate(
            ((lattice_hbm, lattice), (rot_hbm, ya.at[yy]), (home_hbm, home), (shifted_hbm, shifted)))
    ]
    fetch = pltpu.make_async_copy(g.at[0], gv, in_sem.at[4])
    fetch.start()
    for read in reads:
        read.start()

    def greet(s, carry):
        pl.semaphore_signal(barrier, inc=1, device_id=(za, me ^ s), device_id_type=MESH)
        return carry

    lax.fori_loop(1, PB, greet, 0)

    def greet_z(s, carry):
        pl.semaphore_signal(barrier, inc=1, device_id=(za + s, me), device_id_type=MESH)
        return carry

    lax.fori_loop(1, KA - za, greet_z, 0)

    fetch.wait()
    pl.semaphore_wait(barrier, PB - 1 + za)

    def y_copy(s):
        peer = (yy + s) & 7
        return pltpu.make_async_remote_copy(
            rot_hbm, ya.at[yy], y_send.at[s], y_recv.at[yy],
            device_id=(za, peer * 8 + xc), device_id_type=MESH)

    def y_start(s, carry):
        y_copy(s).start()
        return carry

    lax.fori_loop(1, 8, y_start, 0)

    def mate_copy():
        return pltpu.make_async_remote_copy(
            shifted_hbm, mate, c_send.at[1], c_recv.at[1], device_id=(za, me ^ 1), device_id_type=MESH)

    mate_copy().start()

    def g_columns(d):
        return gv.at[:, pl.ds(pl.multiple_of(worker_index(d) * COLS, COLS), COLS)]

    @pl.when(working)
    def _():
        pltpu.make_async_copy(g_columns(me), recv1.at[me], g_recv.at[yy]).start()

    def g_start(step):
        base = ((yy + step) & 7) * 8

        def one(u, carry):
            d = base + (xc ^ u)

            @pl.when(is_worker(d))
            def _():
                pltpu.make_async_remote_copy(
                    g_columns(d), recv1.at[me], g_send.at[0], g_recv.at[yy],
                    device_id=(za, d), device_id_type=MESH).start()

            return carry

        lax.fori_loop(0 if step else 1, 8, one, 0)

    for step in Y_ORDER[:EARLY]:
        g_start(step)

    def y_wait(s, carry):
        src = (yy + s) & 7
        pltpu.make_async_remote_copy(
            rot_hbm, ya.at[src], y_send.at[s], y_recv.at[src],
            device_id=(za, src * 8 + xc), device_id_type=MESH).wait_recv()
        return carry

    lax.fori_loop(1, 8, y_wait, 0)
    reads[1].wait()

    line = jnp.concatenate([ya[y] for y in range(8)], axis=0)
    xb[xx] = jnp.concatenate([line[:, :256], line[:, 256:]], axis=0).astype(BF16)

    def x_copy(s, slot):
        peer = (xx + s) & 3
        return pltpu.make_async_remote_copy(
            xb.at[xx], xb.at[slot], x_send.at[s], x_recv.at[slot],
            device_id=(za, yy * 8 + peer * 2 + cc), device_id_type=MESH)

    for s in range(1, 4):
        x_copy(s, xx).start()
    for step in Y_ORDER[EARLY:]:
        g_start(step)

    def greet_lower(s, carry):
        pl.semaphore_signal(above, inc=1, device_id=(za - s, me), device_id_type=MESH)
        return carry

    lax.fori_loop(1, za + 1, greet_lower, 0)

    for read in reads[:1] + reads[2:]:
        read.wait()

    lane3 = iota((3, 128), 1)
    for tile in range(16):
        a, off = (120 * tile) // 128, (120 * tile) % 128
        b = min(a + 1, 14)
        first, second = lattice[:, 128 * a : 128 * a + 128], lattice[:, 128 * b : 128 * b + 128]
        out = jnp.zeros((3, 128), jnp.int32)
        for c in range(4):
            shift = (2 * c - off) % 128
            here, there = first, second
            if shift:
                here, there = pltpu.roll(first, shift, axis=1), pltpu.roll(second, shift, axis=1)
            value = jnp.where(lane3 < 128 - off + 2 * c, here, there)
            out = jnp.where(lane3 // 32 == c, value, out)
        lat[:, 128 * tile : 128 * tile + 128] = out
    third[...] = iota((8, 2048), 0) * lat[2:3, :]
    xg[...] = jnp.zeros_like(xg)

    def phases(b, carry):
        first = (b >> 2) * lat[0:1, :]
        second = lat[1:2, :]
        k2 = (b & 3) * 2
        low = (first + k2 * second) + third[...]
        high = (first + (k2 + 1) * second) + third[...]
        t = jnp.concatenate([low, high], axis=0)
        rows = pl.ds(pl.multiple_of(b * 16, 16), 16)
        cosines = wave(t).astype(BF16)
        sines = wave(t + 6).astype(BF16)
        for ys in range(8):
            lanes = slice(256 * ys, 256 * ys + 256)
            table[rows, 512 * ys : 512 * ys + 256] = cosines[:, lanes]
            table[rows, 512 * ys + 256 : 512 * ys + 512] = sines[:, lanes]
        return carry

    lax.fori_loop(0, 32, phases, 0)

    for s in range(1, 4):
        x_copy(s, (xx + s) & 3).wait_recv()

    def z_copy(s, slot):
        return pltpu.make_async_remote_copy(
            xb, zc.at[pl.ds(slot * 4, 4)], z_send.at[s], z_recv.at[slot],
            device_id=((za + s) & 7, me), device_id_type=MESH)

    def z_start(s, carry):
        z_copy(s, za).start()
        return carry

    @pl.when(za < KA - 1)
    def _():
        pl.semaphore_wait(above, KA - 1 - za)

    lax.fori_loop(1, KA, z_start, 0)
    zc[pl.ds(za * 4, 4)] = xb[...]

    def group(step):
        ys = (yy - step) & 7
        arrived = recv1.at[pl.ds(8 * ys, 8)]
        pltpu.make_async_copy(arrived, arrived, g_recv.at[ys]).wait()
        for u in range(8):
            xg[u, 0:ROWS, :] = recv1[ys * 8 + u]
        x = xg[...].reshape(256, COLS)
        x_swapped = swap_parts(x.astype(F32)).astype(BF16)
        lanes = pl.ds(pl.multiple_of(ys * 512, 512), 512)
        total = jnp.dot(
            table[:, lanes], jnp.concatenate([x, x_swapped], axis=0), preferred_element_type=F32)
        if step == Y_ORDER[0]:
            acc[...] = total
        else:
            acc[...] += total

    @pl.when(working)
    def _():
        for step in Y_ORDER:
            group(step)
        slot = worker_index(me)

        for step in B_ORDER:
            base = ((yy + step) & 7) * 8
            rows = acc[pl.ds(pl.multiple_of(base * 8, 64), 64), :]
            for u in range(8):
                part = rows[8 * u : 8 * u + 8]
                send2[base + u] = jnp.concatenate([part[:, :128], part[:, 128:]], axis=0).astype(BF16)

            def one(u, carry):
                d = base + (xc ^ (u ^ 4))
                pltpu.make_async_remote_copy(
                    send2.at[d], blk_out.at[slot], b_send.at[0], b_recv.at[0],
                    device_id=(za, d), device_id_type=MESH).start()
                return carry

            if step:
                lax.fori_loop(0, 8, one, 0)
            else:
                lax.fori_loop(0, 4, one, 0)
                lax.fori_loop(5, 8, one, 0)
        pltpu.make_async_copy(send2.at[me], blk_out.at[slot], b_recv.at[0]).start()

    def z_wait(s, carry):
        z_copy(s, (za + s) & 7).wait_recv()
        return carry

    lax.fori_loop(1, KA, z_wait, 0)
    mate_copy().wait_recv()
    r = iota((1, K), 1)
    place = (((r & 1) * 8 + (r >> 6)) * 4 + ((r >> 1) & 3)) * 8 + ((r >> 3) & 7)
    sub = iota((8, K), 0)
    sub8 = iota((8, 256), 0)

    def pick(point):
        at = jnp.minimum(jnp.sum(jnp.where(home[...] == point, place, 0)), K - 1)
        block = zc[(at >> 3) & 31].astype(F32)
        here = sub8 == (at & 7) + 8 * ((at >> 8) ^ cc)
        halves = [
            jnp.sum(jnp.where(here, block[8 * h : 8 * h + 8], 0.0), axis=0, keepdims=True) for h in range(2)
        ]
        return jnp.concatenate(halves, axis=1)

    def picked(first, moved):
        own = jnp.zeros((8, K), F32)
        other = jnp.zeros((8, K), F32)
        for k in range(8):
            own = jnp.where(sub == k, pick(first + k), own)
            other = jnp.where(sub == k, pick(moved[:, k : k + 1]), other)
        return jnp.concatenate([own, other], axis=0)

    give[...] = picked((me ^ 1) * 8, mate[...])

    def c_copy():
        return pltpu.make_async_remote_copy(
            give, take, c_send.at[0], c_recv.at[0], device_id=(za, me ^ 1), device_id_type=MESH)

    c_copy().start()
    both = picked(me * 8, shifted[...])
    c_copy().wait_recv()
    both += take[...]
    for jp in range(32):
        pieces = [both[:, 128 * v : 128 * v + 128] for v in range(4)]
        if jp:
            pieces = [pltpu.roll(piece, 128 - jp, axis=1) for piece in pieces]
        lh[16 * jp : 16 * jp + 16, :] = jnp.concatenate(pieces, axis=1).astype(BF16)
    spread = jnp.where(iota((K, 128), 0) == 32 * (iota((K, 128), 1) // 8), 1.0, 0.0).astype(BF16)
    keep = iota((K, 128), 1) % 8 == iota((K, 128), 0) % 8
    full = jnp.where(keep, jnp.dot(lh[...], spread, preferred_element_type=F32), 0.0)
    for jj in range(8):
        for part in range(2):
            a = 16 * (4 * jj + part)
            b = 16 * (4 * jj + 2 + part)
            rows = slice(16 * jj, 16 * jj + 16)
            lanes = slice(128 * part, 128 * part + 128)
            lhs1[rows, lanes] = jnp.concatenate([full[a : a + 8], full[b : b + 8]], axis=0).astype(BF16)
            left = jnp.concatenate([full[a + 8 : a + 16], full[b + 8 : b + 16]], axis=0)
            lhs2[rows, lanes] = (left if part == 0 else -left).astype(BF16)
    outs = [pltpu.make_async_copy(lhs1, lhs1_out, out_sem.at[0]), pltpu.make_async_copy(lhs2, lhs2_out, out_sem.at[1])]
    for out in outs:
        out.start()

    def y_left(s, carry):
        y_copy(s).wait_send()
        return carry

    lax.fori_loop(1, 8, y_left, 0)
    for s in range(1, 4):
        x_copy(s, xx).wait_send()

    def z_left(s, carry):
        z_copy(s, za).wait_send()
        return carry

    lax.fori_loop(1, KA, z_left, 0)
    c_copy().wait_send()
    mate_copy().wait_send()

    @pl.when(working)
    def _():
        sent = recv1.at[pl.ds(0, WORKERS - 1)]
        pltpu.make_async_copy(sent, sent, g_send.at[0]).wait()
        sent = send2.at[pl.ds(0, PB - 1)]
        pltpu.make_async_copy(sent, sent, b_send.at[0]).wait()

    @pl.when(jnp.logical_not(working))
    def _():
        sent = recv1.at[pl.ds(0, WORKERS)]
        pltpu.make_async_copy(sent, sent, g_send.at[0]).wait()

    for out in outs:
        out.wait()
    pltpu.make_async_copy(blk_out, blk_out, b_recv.at[0]).wait()


def rotate_kernel(
    blk_hbm, lhs1_hbm, lhs2_hbm, counts_hbm, out, blk, lhs1, lhs2, counts, padded, middle, final, in_sem
):
    reads = [
        pltpu.make_async_copy(source, target, in_sem.at[i])
        for i, (source, target) in enumerate(
            ((blk_hbm, blk), (lhs1_hbm, lhs1), (lhs2_hbm, lhs2), (counts_hbm, counts)))
    ]
    for read in reads:
        read.start()
    lane = iota((8, 128), 1)
    low_half = lane < 64

    def compact_tile(t):
        return blk[t // 2].astype(F32)[8 * (t % 2) : 8 * (t % 2) + 8]

    reads[0].wait()
    tiles = [compact_tile(t) for t in range(108)]

    def turn(x, shift):
        shift %= 128
        return pltpu.roll(x, shift, axis=1) if shift else x

    for n in range(NW):
        for mp in range(8):
            halves = []
            for h in range(2):
                start = VEC * (16 * (2 * mp + h) + n)
                t, off = start // 128, start % 128
                piece = turn(tiles[t], 64 * h - off)
                if off + VEC > 128:
                    spill = turn(tiles[t + 1], 64 * h - off)
                    piece = jnp.where(lane < 128 - off + 64 * h, piece, spill)
                halves.append(piece)
            padded[8 * n : 8 * n + 8, 128 * mp : 128 * mp + 128] = jnp.where(low_half, halves[0], halves[1])

    reads[1].wait()
    for p in range(4):
        lanes = slice(256 * p, 256 * p + 256)
        x = padded[:, lanes]
        rhs = jnp.concatenate([x, swap_parts(x)], axis=0).astype(BF16)
        middle[:, lanes] = jnp.dot(lhs1[...], rhs, preferred_element_type=F32)

    for a in range(8):
        for b in range(8):
            lanes = slice(128 * b, 128 * b + 128)
            first = middle[16 * a : 16 * a + 8, lanes]
            second = middle[16 * a + 8 : 16 * a + 16, lanes]
            place = slice(128 * a, 128 * a + 128)
            padded[16 * b : 16 * b + 8, place] = jnp.where(low_half, first, turn(second, 64))
            padded[16 * b + 8 : 16 * b + 16, place] = jnp.where(low_half, turn(first, 64), second)

    reads[2].wait()
    reads[3].wait()
    sub = iota((8, 1), 0)
    limit = jnp.zeros((8, 1), jnp.int32)
    for k in range(8):
        limit = jnp.where(sub == k, counts[0, k], limit)
    row = iota((128, 256), 0)
    limits = jnp.concatenate([jnp.broadcast_to(limit, (8, 256))] * 16, axis=0)
    for p in range(4):
        lanes = slice(256 * p, 256 * p + 256)
        x = padded[:, lanes]
        x = jnp.concatenate([x, swap_parts(x)], axis=0)
        upper = x.astype(BF16)
        lower = (x - upper.astype(F32)).astype(BF16)
        total = jnp.dot(lhs2[...], upper, preferred_element_type=F32)
        total += jnp.dot(lhs2[...], lower, preferred_element_type=F32)
        band = jnp.maximum(row // 8, 4 * p + iota((128, 256), 1) // 64)
        final[:, lanes] = jnp.where(band < limits, total, 0.0)

    for t in range(108):
        begin = 128 * t
        value = None
        for q in range(begin // VEC, (begin + 127) // VEC + 1):
            if q >= 256:
                continue
            i, j = q // 16, q % 16
            at = VEC * q - begin
            piece = turn(final[8 * i : 8 * i + 8, 128 * (j // 2) : 128 * (j // 2) + 128], at - 64 * (j % 2))
            value = piece if value is None else jnp.where(lane < at, value, piece)
        out[0, :, begin : begin + 128] = value.astype(BF16)


def per_device(wannier_g, rotations, home_rows, shifted, band_count, lattice):
    vmem = pl.BlockSpec(memory_space=pltpu.VMEM)
    hbm = pl.BlockSpec(memory_space=pltpu.HBM)
    dma = pltpu.SemaphoreType.DMA
    blocks, lhs1, lhs2 = pl.pallas_call(
        comm_kernel,
        out_shape=(
            jax.ShapeDtypeStruct((WORKERS, 16, 128), BF16),
            jax.ShapeDtypeStruct((128, 256), BF16),
            jax.ShapeDtypeStruct((128, 256), BF16),
        ),
        in_specs=[hbm] * 5,
        out_specs=(hbm, hbm, hbm),
        scratch_shapes=[
            pltpu.VMEM((ROWS, NW * NW * VEC), BF16),
            pltpu.VMEM((1, K), jnp.int32),
            pltpu.VMEM((1, 8), jnp.int32),
            pltpu.VMEM((3, 1920), jnp.int32),
            pltpu.VMEM((PB, ROWS, COLS), BF16),
            pltpu.VMEM((8, 32, COLS), BF16),
            pltpu.VMEM((K, COLS), F32),
            pltpu.VMEM((K, 4096), BF16),
            pltpu.VMEM((PB, 16, 128), BF16),
            pltpu.VMEM((8, 1, 512), F32),
            pltpu.VMEM((4, 16, 256), BF16),
            pltpu.VMEM((32, 16, 256), BF16),
            pltpu.VMEM((3, 2048), jnp.int32),
            pltpu.VMEM((8, 2048), jnp.int32),
            pltpu.VMEM((K, 512), BF16),
            pltpu.VMEM((128, 256), BF16),
            pltpu.VMEM((128, 256), BF16),
            pltpu.VMEM((1, 8), jnp.int32),
            pltpu.VMEM((16, K), F32),
            pltpu.VMEM((16, K), F32),
            dma((5,)), dma((1,)), dma((8,)), dma((1,)), dma((1,)),
            dma((8,)), dma((8,)), dma((4,)), dma((4,)), dma((8,)), dma((8,)), dma((2,)), dma((2,)), dma((2,)),
            pltpu.SemaphoreType.REGULAR,
        ],
        compiler_params=pltpu.CompilerParams(
            collective_id=0, has_side_effects=True, vmem_limit_bytes=60 * 1024 * 1024
        ),
        name="exchange",
    )(wannier_g, rotations, home_rows.reshape(1, K), shifted, lattice)
    return pl.pallas_call(
        rotate_kernel,
        out_shape=jax.ShapeDtypeStruct((1, 8, NW * NW * VEC), BF16),
        in_specs=[hbm] * 4,
        out_specs=vmem,
        scratch_shapes=[
            pltpu.VMEM((WORKERS, 16, 128), BF16),
            pltpu.VMEM((128, 256), BF16),
            pltpu.VMEM((128, 256), BF16),
            pltpu.SMEM((1, 8), jnp.int32),
            pltpu.VMEM((128, 1024), F32),
            pltpu.VMEM((128, 1024), F32),
            pltpu.VMEM((128, 1024), F32),
            dma((4,)),
        ],
        compiler_params=pltpu.CompilerParams(vmem_limit_bytes=60 * 1024 * 1024),
        name="rotate",
    )(blocks, lhs1, lhs2, band_count)


def solution(mesh):
    placed = (P("ka", "pb", None), P(("ka", "pb"), None), P(), P("ka", "pb"), P("ka", "pb"), P())
    return jax.shard_map(
        per_device, mesh=mesh, in_specs=placed, out_specs=P("ka", "pb", None), check_vma=False
    )
```

```python
import jax
import jax.numpy as jnp
from jax import lax
from jax.experimental import pallas as pl
from jax.experimental.pallas import tpu as pltpu
from jax.sharding import PartitionSpec as P

NW = 16
NKG = 8
K = 512
VEC = 54
ROWS = 30
PB = 64
KA = 8
Y_ORDER = (2, 6, 3, 5, 1, 7, 4, 0)
B_ORDER = (4, 3, 5, 2, 6, 1, 7, 0)
EARLY = 4
WORKERS = 54
COLS = 256
MESH = pl.DeviceIdType.MESH
F32 = jnp.float32
BF16 = jnp.bfloat16
HALF_ROOT = 0.70703125
CUBIC = (0.5 - HALF_ROOT) / 3.0
LINEAR = HALF_ROOT - CUBIC


def worker_index(d):
    return (27 * d + 31) >> 5


def is_worker(d):
    return ((5 * d) & 31) < 27


def iota(shape, axis):
    return lax.broadcasted_iota(jnp.int32, shape, axis)


def swap_parts(x):
    width = x.shape[1]
    even = iota(x.shape, 1) % 2 == 0
    return jnp.where(even, -pltpu.roll(x, width - 1, axis=1), pltpu.roll(x, 1, axis=1))


def wave(t):
    w = (jnp.abs((t & 7) - 4) - 2).astype(F32)
    return w * (LINEAR + CUBIC * (w * w))


def comm_kernel(
    g, rot_hbm, home_hbm, shifted_hbm, lattice_hbm, blk_out, lhs1_out, lhs2_out,
    gv, home, shifted, lattice, recv1, xg, acc, table, send2, ya, xb, zc, lat, third, lh, lhs1, lhs2, mate, give, take,
    in_sem, g_send, g_recv, b_send, b_recv, y_send, y_recv, x_send, x_recv, z_send, z_recv, c_send, c_recv, out_sem, above,
):
    za = lax.axis_index("ka")
    me = lax.axis_index("pb")
    yy = me >> 3
    xc = me & 7
    xx = xc >> 1
    cc = xc & 1
    working = is_worker(me)
    barrier = pltpu.get_barrier_semaphore()
    reads = [
        pltpu.make_async_copy(source, target, in_sem.at[i])
        for i, (source, target) in enumerate(
            ((lattice_hbm, lattice), (rot_hbm, ya.at[yy]), (home_hbm, home), (shifted_hbm, shifted)))
    ]
    fetch = pltpu.make_async_copy(g.at[0], gv, in_sem.at[4])
    fetch.start()
    for read in reads:
        read.start()

    def greet(s, carry):
        pl.semaphore_signal(barrier, inc=1, device_id=(za, me ^ s), device_id_type=MESH)
        return carry

    lax.fori_loop(1, PB, greet, 0)

    def greet_z(s, carry):
        pl.semaphore_signal(barrier, inc=1, device_id=(za + s, me), device_id_type=MESH)
        return carry

    lax.fori_loop(1, KA - za, greet_z, 0)

    fetch.wait()
    pl.semaphore_wait(barrier, PB - 1 + za)

    def y_copy(s):
        peer = (yy + s) & 7
        return pltpu.make_async_remote_copy(
            rot_hbm, ya.at[yy], y_send.at[s], y_recv.at[yy],
            device_id=(za, peer * 8 + xc), device_id_type=MESH)

    def y_start(s, carry):
        y_copy(s).start()
        return carry

    lax.fori_loop(1, 8, y_start, 0)

    def mate_copy():
        return pltpu.make_async_remote_copy(
            shifted_hbm, mate, c_send.at[1], c_recv.at[1], device_id=(za, me ^ 1), device_id_type=MESH)

    mate_copy().start()

    def g_columns(d):
        return gv.at[:, pl.ds(pl.multiple_of(worker_index(d) * COLS, COLS), COLS)]

    @pl.when(working)
    def _():
        pltpu.make_async_copy(g_columns(me), recv1.at[me], g_recv.at[yy]).start()

    def g_start(step):
        base = ((yy + step) & 7) * 8

        def one(u, carry):
            d = base + (xc ^ u)

            @pl.when(is_worker(d))
            def _():
                pltpu.make_async_remote_copy(
                    g_columns(d), recv1.at[me], g_send.at[0], g_recv.at[yy],
                    device_id=(za, d), device_id_type=MESH).start()

            return carry

        lax.fori_loop(0 if step else 1, 8, one, 0)

    for step in Y_ORDER[:EARLY]:
        g_start(step)

    def y_wait(s, carry):
        src = (yy + s) & 7
        pltpu.make_async_remote_copy(
            rot_hbm, ya.at[src], y_send.at[s], y_recv.at[src],
            device_id=(za, src * 8 + xc), device_id_type=MESH).wait_recv()
        return carry

    lax.fori_loop(1, 8, y_wait, 0)
    reads[1].wait()

    line = jnp.concatenate([ya[y] for y in range(8)], axis=0)
    xb[xx] = jnp.concatenate([line[:, :256], line[:, 256:]], axis=0).astype(BF16)

    def x_copy(s, slot):
        peer = (xx + s) & 3
        return pltpu.make_async_remote_copy(
            xb.at[xx], xb.at[slot], x_send.at[s], x_recv.at[slot],
            device_id=(za, yy * 8 + peer * 2 + cc), device_id_type=MESH)

    for s in range(1, 4):
        x_copy(s, xx).start()
    for step in Y_ORDER[EARLY:]:
        g_start(step)

    def greet_lower(s, carry):
        pl.semaphore_signal(above, inc=1, device_id=(za - s, me), device_id_type=MESH)
        return carry

    lax.fori_loop(1, za + 1, greet_lower, 0)

    for read in reads[:1] + reads[2:]:
        read.wait()

    lane3 = iota((3, 128), 1)
    for tile in range(16):
        a, off = (120 * tile) // 128, (120 * tile) % 128
        b = min(a + 1, 14)
        first, second = lattice[:, 128 * a : 128 * a + 128], lattice[:, 128 * b : 128 * b + 128]
        out = jnp.zeros((3, 128), jnp.int32)
        for c in range(4):
            shift = (2 * c - off) % 128
            here, there = first, second
            if shift:
                here, there = pltpu.roll(first, shift, axis=1), pltpu.roll(second, shift, axis=1)
            value = jnp.where(lane3 < 128 - off + 2 * c, here, there)
            out = jnp.where(lane3 // 32 == c, value, out)
        lat[:, 128 * tile : 128 * tile + 128] = out
    third[...] = iota((8, 2048), 0) * lat[2:3, :]
    xg[...] = jnp.zeros_like(xg)

    def phases(b, carry):
        first = (b >> 2) * lat[0:1, :]
        second = lat[1:2, :]
        k2 = (b & 3) * 2
        low = (first + k2 * second) + third[...]
        high = (first + (k2 + 1) * second) + third[...]
        t = jnp.concatenate([low, high], axis=0)
        rows = pl.ds(pl.multiple_of(b * 16, 16), 16)
        cosines = wave(t).astype(BF16)
        sines = wave(t + 6).astype(BF16)
        for ys in range(8):
            lanes = slice(256 * ys, 256 * ys + 256)
            table[rows, 512 * ys : 512 * ys + 256] = cosines[:, lanes]
            table[rows, 512 * ys + 256 : 512 * ys + 512] = sines[:, lanes]
        return carry

    lax.fori_loop(0, 32, phases, 0)

    for s in range(1, 4):
        x_copy(s, (xx + s) & 3).wait_recv()

    def z_copy(s, slot):
        return pltpu.make_async_remote_copy(
            xb, zc.at[pl.ds(slot * 4, 4)], z_send.at[s], z_recv.at[slot],
            device_id=((za + s) & 7, me), device_id_type=MESH)

    def z_start(s, carry):
        z_copy(s, za).start()
        return carry

    @pl.when(za < KA - 1)
    def _():
        pl.semaphore_wait(above, KA - 1 - za)

    lax.fori_loop(1, KA, z_start, 0)
    zc[pl.ds(za * 4, 4)] = xb[...]

    def group(step):
        ys = (yy - step) & 7
        arrived = recv1.at[pl.ds(8 * ys, 8)]
        pltpu.make_async_copy(arrived, arrived, g_recv.at[ys]).wait()
        for u in range(8):
            xg[u, 0:ROWS, :] = recv1[ys * 8 + u]
        x = xg[...].reshape(256, COLS)
        x_swapped = swap_parts(x.astype(F32)).astype(BF16)
        lanes = pl.ds(pl.multiple_of(ys * 512, 512), 512)
        total = jnp.dot(
            table[:, lanes], jnp.concatenate([x, x_swapped], axis=0), preferred_element_type=F32)
        if step == Y_ORDER[0]:
            acc[...] = total
        else:
            acc[...] += total

    @pl.when(working)
    def _():
        for step in Y_ORDER:
            group(step)
        slot = worker_index(me)

        for step in B_ORDER:
            base = ((yy + step) & 7) * 8
            rows = acc[pl.ds(pl.multiple_of(base * 8, 64), 64), :]
            for u in range(8):
                part = rows[8 * u : 8 * u + 8]
                send2[base + u] = jnp.concatenate([part[:, :128], part[:, 128:]], axis=0).astype(BF16)

            def one(u, carry):
                d = base + (xc ^ (u ^ (4 + 2 * (u >> 2))))
                pltpu.make_async_remote_copy(
                    send2.at[d], blk_out.at[slot], b_send.at[0], b_recv.at[0],
                    device_id=(za, d), device_id_type=MESH).start()
                return carry

            if step:
                lax.fori_loop(0, 8, one, 0)
            else:
                lax.fori_loop(0, 6, one, 0)
                lax.fori_loop(7, 8, one, 0)
        pltpu.make_async_copy(send2.at[me], blk_out.at[slot], b_recv.at[0]).start()

    def z_wait(s, carry):
        z_copy(s, (za + s) & 7).wait_recv()
        return carry

    lax.fori_loop(1, KA, z_wait, 0)
    mate_copy().wait_recv()
    r = iota((1, K), 1)
    place = (((r & 1) * 8 + (r >> 6)) * 4 + ((r >> 1) & 3)) * 8 + ((r >> 3) & 7)
    sub = iota((8, K), 0)
    sub8 = iota((8, 256), 0)

    def pick(point):
        at = jnp.minimum(jnp.sum(jnp.where(home[...] == point, place, 0)), K - 1)
        block = zc[(at >> 3) & 31].astype(F32)
        here = sub8 == (at & 7) + 8 * ((at >> 8) ^ cc)
        halves = [
            jnp.sum(jnp.where(here, block[8 * h : 8 * h + 8], 0.0), axis=0, keepdims=True) for h in range(2)
        ]
        return jnp.concatenate(halves, axis=1)

    def picked(first, moved):
        own = jnp.zeros((8, K), F32)
        other = jnp.zeros((8, K), F32)
        for k in range(8):
            own = jnp.where(sub == k, pick(first + k), own)
            other = jnp.where(sub == k, pick(moved[:, k : k + 1]), other)
        return jnp.concatenate([own, other], axis=0)

    give[...] = picked((me ^ 1) * 8, mate[...])

    def c_copy():
        return pltpu.make_async_remote_copy(
            give, take, c_send.at[0], c_recv.at[0], device_id=(za, me ^ 1), device_id_type=MESH)

    c_copy().start()
    both = picked(me * 8, shifted[...])
    c_copy().wait_recv()
    both += take[...]
    for jp in range(32):
        pieces = [both[:, 128 * v : 128 * v + 128] for v in range(4)]
        if jp:
            pieces = [pltpu.roll(piece, 128 - jp, axis=1) for piece in pieces]
        lh[16 * jp : 16 * jp + 16, :] = jnp.concatenate(pieces, axis=1).astype(BF16)
    spread = jnp.where(iota((K, 128), 0) == 32 * (iota((K, 128), 1) // 8), 1.0, 0.0).astype(BF16)
    keep = iota((K, 128), 1) % 8 == iota((K, 128), 0) % 8
    full = jnp.where(keep, jnp.dot(lh[...], spread, preferred_element_type=F32), 0.0)
    for jj in range(8):
        for part in range(2):
            a = 16 * (4 * jj + part)
            b = 16 * (4 * jj + 2 + part)
            rows = slice(16 * jj, 16 * jj + 16)
            lanes = slice(128 * part, 128 * part + 128)
            lhs1[rows, lanes] = jnp.concatenate([full[a : a + 8], full[b : b + 8]], axis=0).astype(BF16)
            left = jnp.concatenate([full[a + 8 : a + 16], full[b + 8 : b + 16]], axis=0)
            lhs2[rows, lanes] = (left if part == 0 else -left).astype(BF16)
    outs = [pltpu.make_async_copy(lhs1, lhs1_out, out_sem.at[0]), pltpu.make_async_copy(lhs2, lhs2_out, out_sem.at[1])]
    for out in outs:
        out.start()

    def y_left(s, carry):
        y_copy(s).wait_send()
        return carry

    lax.fori_loop(1, 8, y_left, 0)
    for s in range(1, 4):
        x_copy(s, xx).wait_send()

    def z_left(s, carry):
        z_copy(s, za).wait_send()
        return carry

    lax.fori_loop(1, KA, z_left, 0)
    c_copy().wait_send()
    mate_copy().wait_send()

    @pl.when(working)
    def _():
        sent = recv1.at[pl.ds(0, WORKERS - 1)]
        pltpu.make_async_copy(sent, sent, g_send.at[0]).wait()
        sent = send2.at[pl.ds(0, PB - 1)]
        pltpu.make_async_copy(sent, sent, b_send.at[0]).wait()

    @pl.when(jnp.logical_not(working))
    def _():
        sent = recv1.at[pl.ds(0, WORKERS)]
        pltpu.make_async_copy(sent, sent, g_send.at[0]).wait()

    for out in outs:
        out.wait()
    pltpu.make_async_copy(blk_out, blk_out, b_recv.at[0]).wait()


def rotate_kernel(
    blk_hbm, lhs1_hbm, lhs2_hbm, counts_hbm, out, blk, lhs1, lhs2, counts, padded, middle, final, in_sem
):
    reads = [
        pltpu.make_async_copy(source, target, in_sem.at[i])
        for i, (source, target) in enumerate(
            ((blk_hbm, blk), (lhs1_hbm, lhs1), (lhs2_hbm, lhs2), (counts_hbm, counts)))
    ]
    for read in reads:
        read.start()
    lane = iota((8, 128), 1)
    low_half = lane < 64

    def compact_tile(t):
        return blk[t // 2].astype(F32)[8 * (t % 2) : 8 * (t % 2) + 8]

    reads[0].wait()
    tiles = [compact_tile(t) for t in range(108)]

    def turn(x, shift):
        shift %= 128
        return pltpu.roll(x, shift, axis=1) if shift else x

    for n in range(NW):
        for mp in range(8):
            halves = []
            for h in range(2):
                start = VEC * (16 * (2 * mp + h) + n)
                t, off = start // 128, start % 128
                piece = turn(tiles[t], 64 * h - off)
                if off + VEC > 128:
                    spill = turn(tiles[t + 1], 64 * h - off)
                    piece = jnp.where(lane < 128 - off + 64 * h, piece, spill)
                halves.append(piece)
            padded[8 * n : 8 * n + 8, 128 * mp : 128 * mp + 128] = jnp.where(low_half, halves[0], halves[1])

    reads[1].wait()
    for p in range(4):
        lanes = slice(256 * p, 256 * p + 256)
        x = padded[:, lanes]
        rhs = jnp.concatenate([x, swap_parts(x)], axis=0).astype(BF16)
        middle[:, lanes] = jnp.dot(lhs1[...], rhs, preferred_element_type=F32)

    for a in range(8):
        for b in range(8):
            lanes = slice(128 * b, 128 * b + 128)
            first = middle[16 * a : 16 * a + 8, lanes]
            second = middle[16 * a + 8 : 16 * a + 16, lanes]
            place = slice(128 * a, 128 * a + 128)
            padded[16 * b : 16 * b + 8, place] = jnp.where(low_half, first, turn(second, 64))
            padded[16 * b + 8 : 16 * b + 16, place] = jnp.where(low_half, turn(first, 64), second)

    reads[2].wait()
    reads[3].wait()
    sub = iota((8, 1), 0)
    limit = jnp.zeros((8, 1), jnp.int32)
    for k in range(8):
        limit = jnp.where(sub == k, counts[0, k], limit)
    row = iota((128, 256), 0)
    limits = jnp.concatenate([jnp.broadcast_to(limit, (8, 256))] * 16, axis=0)
    for p in range(4):
        lanes = slice(256 * p, 256 * p + 256)
        x = padded[:, lanes]
        x = jnp.concatenate([x, swap_parts(x)], axis=0)
        upper = x.astype(BF16)
        lower = (x - upper.astype(F32)).astype(BF16)
        total = jnp.dot(lhs2[...], upper, preferred_element_type=F32)
        total += jnp.dot(lhs2[...], lower, preferred_element_type=F32)
        band = jnp.maximum(row // 8, 4 * p + iota((128, 256), 1) // 64)
        final[:, lanes] = jnp.where(band < limits, total, 0.0)

    for t in range(108):
        begin = 128 * t
        value = None
        for q in range(begin // VEC, (begin + 127) // VEC + 1):
            if q >= 256:
                continue
            i, j = q // 16, q % 16
            at = VEC * q - begin
            piece = turn(final[8 * i : 8 * i + 8, 128 * (j // 2) : 128 * (j // 2) + 128], at - 64 * (j % 2))
            value = piece if value is None else jnp.where(lane < at, value, piece)
        out[0, :, begin : begin + 128] = value.astype(BF16)


def per_device(wannier_g, rotations, home_rows, shifted, band_count, lattice):
    vmem = pl.BlockSpec(memory_space=pltpu.VMEM)
    hbm = pl.BlockSpec(memory_space=pltpu.HBM)
    dma = pltpu.SemaphoreType.DMA
    blocks, lhs1, lhs2 = pl.pallas_call(
        comm_kernel,
        out_shape=(
            jax.ShapeDtypeStruct((WORKERS, 16, 128), BF16),
            jax.ShapeDtypeStruct((128, 256), BF16),
            jax.ShapeDtypeStruct((128, 256), BF16),
        ),
        in_specs=[hbm] * 5,
        out_specs=(hbm, hbm, hbm),
        scratch_shapes=[
            pltpu.VMEM((ROWS, NW * NW * VEC), BF16),
            pltpu.VMEM((1, K), jnp.int32),
            pltpu.VMEM((1, 8), jnp.int32),
            pltpu.VMEM((3, 1920), jnp.int32),
            pltpu.VMEM((PB, ROWS, COLS), BF16),
            pltpu.VMEM((8, 32, COLS), BF16),
            pltpu.VMEM((K, COLS), F32),
            pltpu.VMEM((K, 4096), BF16),
            pltpu.VMEM((PB, 16, 128), BF16),
            pltpu.VMEM((8, 1, 512), F32),
            pltpu.VMEM((4, 16, 256), BF16),
            pltpu.VMEM((32, 16, 256), BF16),
            pltpu.VMEM((3, 2048), jnp.int32),
            pltpu.VMEM((8, 2048), jnp.int32),
            pltpu.VMEM((K, 512), BF16),
            pltpu.VMEM((128, 256), BF16),
            pltpu.VMEM((128, 256), BF16),
            pltpu.VMEM((1, 8), jnp.int32),
            pltpu.VMEM((16, K), F32),
            pltpu.VMEM((16, K), F32),
            dma((5,)), dma((1,)), dma((8,)), dma((1,)), dma((1,)),
            dma((8,)), dma((8,)), dma((4,)), dma((4,)), dma((8,)), dma((8,)), dma((2,)), dma((2,)), dma((2,)),
            pltpu.SemaphoreType.REGULAR,
        ],
        compiler_params=pltpu.CompilerParams(
            collective_id=0, has_side_effects=True, vmem_limit_bytes=60 * 1024 * 1024
        ),
        name="exchange",
    )(wannier_g, rotations, home_rows.reshape(1, K), shifted, lattice)
    return pl.pallas_call(
        rotate_kernel,
        out_shape=jax.ShapeDtypeStruct((1, 8, NW * NW * VEC), BF16),
        in_specs=[hbm] * 4,
        out_specs=vmem,
        scratch_shapes=[
            pltpu.VMEM((WORKERS, 16, 128), BF16),
            pltpu.VMEM((128, 256), BF16),
            pltpu.VMEM((128, 256), BF16),
            pltpu.SMEM((1, 8), jnp.int32),
            pltpu.VMEM((128, 1024), F32),
            pltpu.VMEM((128, 1024), F32),
            pltpu.VMEM((128, 1024), F32),
            dma((4,)),
        ],
        compiler_params=pltpu.CompilerParams(vmem_limit_bytes=60 * 1024 * 1024),
        name="rotate",
    )(blocks, lhs1, lhs2, band_count)


def solution(mesh):
    placed = (P("ka", "pb", None), P(("ka", "pb"), None), P(), P("ka", "pb"), P("ka", "pb"), P())
    return jax.shard_map(
        per_device, mesh=mesh, in_specs=placed, out_specs=P("ka", "pb", None), check_vma=False
    )
```
